128 devices in a mesh: fsdp: 4 (over y), tok: 32 (over x, z, core).
Axes of the slice: x: 4, y: 4, z: 4, core: 2. Of those that a mesh axis runs over, the one named last changes fastest.
Arguments:
- tokens: bfloat16 [32768, 8192], P(('fsdp', 'tok')), may hold values from -6 to 6
- frozen_value_weight: bfloat16 [8192, 1024], P(None, 'fsdp'), may hold values from -0.0625 to 0.0625
- adapter_down_maps: bfloat16 [8192, 4096], P('tok', 'fsdp'), may hold values from -0.0625 to 0.0625
- adapter_up_maps: bfloat16 [1024, 4096], P('tok', 'fsdp'), may hold values from -1.5 to 1.5
- cotangent: bfloat16 [32768, 1024], P(('fsdp', 'tok')), may hold values from -6 to 6
- packing_block_tenant: int32 [256], replicated, may hold values from 0 to 255
- packing_block_fill: int32 [256], replicated, may hold values from 1 to 128
Outputs:
- values: bfloat16 [32768, 1024], P(('fsdp', 'tok'))
- token_gradient: bfloat16 [32768, 8192], P(('fsdp', 'tok'))
- grad_down: float32 [8192, 4096], P('tok', 'fsdp')
- grad_up: float32 [1024, 4096], P('tok', 'fsdp')
The draws below stay inside these ranges and needn't reach their ends.
All inputs are finite; a program needn't handle non-finite values.
Results may differ from the reference program's by a relative error of at most 0.0055.
Values may be sent and summed in bfloat16 or wider, within the bound.
A program may use at most 128 MiB of HBM per device.

```python
import math
import jax
import jax.numpy as jnp
import numpy as np
from jax import lax

MODEL_WIDTH = 8192
VALUE_WIDTH = 1024
ADAPTER_RANK = 16
TENANT_COUNT = 256
BLOCK = 128
TOKENS = 32768
BLOCKS = 256


def draw_packing_block_fill(key, part):
    key = jax.random.fold_in(key, 7)
    fill_key, chosen_key = jax.random.split(key)
    fill_values = jax.random.randint(fill_key, (BLOCKS,), 1, BLOCK + 1)
    chosen = jax.random.randint(chosen_key, (), 0, BLOCKS)
    positions = jnp.arange(BLOCKS)
    fill_values = jnp.where(positions == chosen, BLOCK, fill_values)
    fill_values = jnp.where(positions == (chosen + BLOCKS // 2) % BLOCKS, 1, fill_values)
    return fill_values.astype(jnp.int32)


def plant(drawn, own_key, least, high):
    shape = drawn.shape
    place = [jax.random.randint(jax.random.fold_in(own_key, axis), (), 0, shape[axis]) for axis in range(len(shape))]
    drawn = drawn.at[tuple(place)].set(least)
    longest = shape.index(max(shape))
    place[longest] = (place[longest] + 1) % shape[longest]
    return drawn.at[tuple(place)].set(high)


def block_levels(own_key, dims, cuts, smallest, largest):
    def one(position, parts):
        heights = jax.random.uniform(jax.random.fold_in(jax.random.fold_in(own_key, 6), position), (parts,), jnp.float32, smallest / len(cuts), largest / len(cuts))
        return jnp.repeat(jnp.exp(heights), dims[position] // parts).reshape((-1,) + (1,) * (len(dims) - position - 1))

    loudness = one(*cuts[0])
    for cut in cuts[1:]:
        loudness = loudness * one(*cut)
    return loudness


def rank_bounds(count, lean):
    loads = [(1 << 20) // math.isqrt(rank ** lean) + 1 for rank in range(1, count + 1)]
    spread = 1 + sum(loads) // (1 << 30)
    return np.cumsum(np.array([max(1, weight // spread) for weight in loads]))


def skewed_ids(rng, extent, number_of, skew):
    grid = rank_bounds(number_of, skew)
    lot = jax.random.randint(jax.random.fold_in(rng, 1), extent, 0, int(grid[number_of - 1]))
    rank = jnp.searchsorted(jnp.asarray(grid, jnp.int32), lot, side="right")
    return jax.random.permutation(jax.random.fold_in(rng, 2), number_of)[rank].astype(jnp.int32)


def scatter_about(stream_key, shape, width, bound, shards=(), kind=jnp.bfloat16):
    entries = jax.random.normal(stream_key, shape, jnp.float32) * width
    if len(shards) > 0:
        entries = block_levels(stream_key, shape, shards, -0.22, 0.18) * entries
    return jnp.clip(entries, min=-bound, max=bound).astype(kind)


def setup_inputs(seed: int = 0) -> dict:
    streams_of = jax.random.split(jax.random.key(seed), 8)
    return {
        "tokens": scatter_about(streams_of[0], (TOKENS, MODEL_WIDTH), 1.0, 6.0, ((0, 128),)),
        "frozen_value_weight": scatter_about(streams_of[1], (MODEL_WIDTH, VALUE_WIDTH), MODEL_WIDTH ** -0.5, 0.0625, ((1, 4),)),
        "adapter_down_maps": scatter_about(streams_of[2], (MODEL_WIDTH, TENANT_COUNT * ADAPTER_RANK), MODEL_WIDTH ** -0.5, 0.0625, ((0, 32), (1, 4))),
        "adapter_up_maps": scatter_about(streams_of[3], (VALUE_WIDTH, TENANT_COUNT * ADAPTER_RANK), ADAPTER_RANK ** -0.5, 1.5, ((0, 32), (1, 4))),
        "cotangent": scatter_about(streams_of[4], (TOKENS, VALUE_WIDTH), 1.0, 6.0, ((0, 128),)),
        "packing_block_tenant": plant(skewed_ids(streams_of[5], (BLOCKS,), TENANT_COUNT, 2), jax.random.fold_in(streams_of[5], 3), 0, TENANT_COUNT - 1).astype(jnp.int32),
        "packing_block_fill": draw_packing_block_fill(jax.random.fold_in(streams_of[7], 71), 0),
    }


ADAPTER_SCALE = 2.0


def reference(tokens, frozen_value_weight, adapter_down_maps, adapter_up_maps, cotangent, packing_block_tenant, packing_block_fill):
    filled_row_count = tokens.shape[0]
    blocks = filled_row_count // BLOCK
    used_rows = (jnp.arange(BLOCK, dtype=jnp.int32)[None, :] < packing_block_fill[:, None]).reshape(filled_row_count, 1)
    grad_out = cotangent * used_rows.astype(cotangent.dtype)
    feature_blocks = tokens.reshape(blocks, BLOCK, MODEL_WIDTH)
    gradient_blocks = grad_out.reshape(blocks, BLOCK, VALUE_WIDTH)

    def per_block_step(totals, inputs_now):
        down_gradient_total, up_gradient_total = totals
        feat_rows, grad_rows, tenant = inputs_now
        column_offset = (tenant * ADAPTER_RANK).astype(jnp.int32)
        down_map_columns = lax.dynamic_slice_in_dim(adapter_down_maps, column_offset, ADAPTER_RANK, 1)
        up_map_columns = lax.dynamic_slice_in_dim(adapter_up_maps, column_offset, ADAPTER_RANK, 1)
        rank_space_input = jnp.dot(feat_rows, down_map_columns, preferred_element_type=jnp.float32).astype(jnp.bfloat16)
        rank_space_gradient = (ADAPTER_SCALE * jnp.dot(grad_rows, up_map_columns, preferred_element_type=jnp.float32)).astype(jnp.bfloat16)
        adapter_output = (ADAPTER_SCALE * jnp.dot(rank_space_input, up_map_columns.T, preferred_element_type=jnp.float32)).astype(jnp.bfloat16)
        adapter_backward = jnp.dot(rank_space_gradient, down_map_columns.T, preferred_element_type=jnp.float32).astype(jnp.bfloat16)
        down_term = jnp.dot(feat_rows.T, rank_space_gradient, preferred_element_type=jnp.float32)
        up_term = ADAPTER_SCALE * jnp.dot(grad_rows.T, rank_space_input, preferred_element_type=jnp.float32)
        old_down = lax.dynamic_slice_in_dim(down_gradient_total, column_offset, ADAPTER_RANK, 1)
        down_gradient_total = lax.dynamic_update_slice_in_dim(down_gradient_total, old_down + down_term, column_offset, 1)
        old_up = lax.dynamic_slice_in_dim(up_gradient_total, column_offset, ADAPTER_RANK, 1)
        up_gradient_total = lax.dynamic_update_slice_in_dim(up_gradient_total, old_up + up_term, column_offset, 1)
        return (down_gradient_total, up_gradient_total), (adapter_output, adapter_backward)

    initial_totals = (jnp.zeros((MODEL_WIDTH, TENANT_COUNT * ADAPTER_RANK), jnp.float32), jnp.zeros((VALUE_WIDTH, TENANT_COUNT * ADAPTER_RANK), jnp.float32))
    (down_gradient_total, up_gradient_total), (adapter_output, adapter_backward) = lax.scan(per_block_step, initial_totals, (feature_blocks, gradient_blocks, packing_block_tenant))
    masked_token_rows = used_rows.astype(jnp.float32)
    frozen_output = jnp.dot(tokens, frozen_value_weight, preferred_element_type=jnp.float32)
    values = (masked_token_rows * (frozen_output + adapter_output.reshape(filled_row_count, VALUE_WIDTH).astype(jnp.float32))).astype(jnp.bfloat16)
    frozen_backward = jnp.dot(grad_out, frozen_value_weight.T, preferred_element_type=jnp.float32)
    token_gradient = (frozen_backward + adapter_backward.reshape(filled_row_count, MODEL_WIDTH).astype(jnp.float32)).astype(jnp.bfloat16)
    counts = jax.ops.segment_sum(packing_block_fill.astype(jnp.float32), packing_block_tenant, num_segments=TENANT_COUNT)
    denominator = jnp.repeat(jnp.maximum(counts, 1.0), ADAPTER_RANK)
    return values, token_gradient, down_gradient_total / denominator, up_gradient_total / denominator
```

```python
import jax
import jax.numpy as jnp
from jax import lax
from jax.experimental import pallas as pl
from jax.experimental.pallas import tpu as pltpu
from jax.sharding import PartitionSpec as P

RANK = 16
BLOCK = 128
SCALE = 2.0
BF = jnp.bfloat16
F32 = jnp.float32
NT = (((1,), (1,)), ((), ()))
TN = (((0,), (0,)), ((), ()))
PANEL = 1152
HALF = 576


def mm(a, b, dims=(((1,), (0,)), ((), ()))):
    return lax.dot_general(a, b, dims, preferred_element_type=F32)


def iota(shape, dim):
    return lax.broadcasted_iota(jnp.int32, shape, dim)


def pick(cond):
    return jnp.where(cond, 1.0, 0.0).astype(BF)


def kernel(
    x_hbm,
    w_hbm,
    panel,
    cot,
    tenant,
    fill,
    where,
    values,
    tgrad,
    gdown,
    gup,
    xv,
    wall,
    go,
    va,
    tga,
    aball,
    send_a,
    vb,
    send_b,
    at,
    recv_b,
    bt,
    gs,
    us,
    ur,
    terms,
    lo,
    rg_s,
    onehot,
    acc,
    cnt,
    loc,
    ab_sem,
    wy_sem,
    wx_sem,
    wc_sem,
    pa_sem,
    pb_sem,
    ga_sem,
    gu_sem,
    gy_sem,
):
    f = lax.axis_index("fsdp")
    t = lax.axis_index("tok")
    x = t // 8
    z = (t // 2) % 4
    c = t % 2

    def up(i, d):
        return lax.rem(i + d, 4)

    def dev_y(d):
        return (up(f, d), t)

    def dev_x(d):
        return (f, up(x, d) * 8 + z * 2 + c)

    def dev_z(d):
        return (f, x * 8 + up(z, d) * 2 + c)

    sibling = (f, x * 8 + z * 2 + (1 - c))

    def remote(src, dst, sem, i, dev):
        return pltpu.make_async_remote_copy(
            src_ref=src,
            dst_ref=dst,
            send_sem=sem.at[0, i],
            recv_sem=sem.at[1, i],
            device_id=dev,
            device_id_type=pl.DeviceIdType.MESH,
        )

    get_x = pltpu.make_async_copy(x_hbm, xv, loc.at[0])
    get_w = pltpu.make_async_copy(w_hbm, wall.at[f], loc.at[1])
    get_p = pltpu.make_async_copy(panel, aball.at[pl.ds(f * 72, 72)], loc.at[2])
    get_p.start()
    get_x.start()
    get_w.start()

    pending = []

    def ring_y(src_of, part_of, sem):
        first = {}
        for i, (d, s) in enumerate(((1, 0), (3, 1), (1, 1), (3, 0))):
            cp = remote(src_of(s), part_of(f, s), sem, i, dev_y(d))
            cp.start()
            first[d, s] = cp
            pending.append(cp)

        def forward():
            out = []
            for i, (d, s) in enumerate(((1, 0), (3, 1))):
                first[d, s].wait_recv()
                src = up(f, 4 - d)
                cp = remote(part_of(src, s), part_of(src, s), sem, 4 + i, dev_y(d))
                cp.start()
                out.append(cp)
                pending.append(cp)
            first[1, 1].wait_recv()
            first[3, 0].wait_recv()
            return out

        return forward

    ab_forward = ring_y(
        lambda s: panel.at[pl.ds(s * 36, 36)],
        lambda i, s: aball.at[pl.ds(i * 72 + s * 36, 36)],
        ab_sem,
    )

    b0 = (f * 32 + t) * 2
    rows = iota((256, 1), 0)
    limit = jnp.where(rows < BLOCK, fill[b0], fill[b0 + 1] + BLOCK)
    used = rows < limit
    for j in range(4):
        go[j] = jnp.where(used, cot[:, j * 256 : (j + 1) * 256].astype(F32), 0.0).astype(BF)
    va[...] = jnp.zeros_like(va)
    get_x.wait()
    get_w.wait()

    def own_step(k, carry):
        cols = pl.ds(pl.multiple_of(k * 256, 256), 256)
        wk = wall[f, cols, :]
        va[f] += mm(xv[:, cols], wk)
        tga[:, cols] = mm(go[f], wk, NT)
        return carry

    lax.fori_loop(0, 32, own_step, 0)

    tlane = (iota((1, 1024), 1) >> 4) + f * 64

    def count_step(b, total):
        return total + jnp.where(tlane == tenant[b], fill[b].astype(F32), 0.0)

    cnt[...] = lax.fori_loop(0, 256, count_step, jnp.zeros((1, 1024), F32))

    ab_last = ab_forward()

    base = (x * 1024 + c * 512, 4096 + z * 1024 + c * 512)

    def wslice(fi, row0):
        return wall.at[fi, pl.ds(pl.multiple_of(row0, 256), 256), :]

    wy = {}
    n_y = 0
    for h in range(2):
        for d, s in ((1, 0), (3, 1), (1, 1), (3, 0)):
            r0 = base[h] + s * 256
            cp = remote(
                w_hbm.at[pl.ds(pl.multiple_of(r0, 256), 256), :],
                wslice(f, r0),
                wy_sem,
                n_y,
                dev_y(d),
            )
            cp.start()
            wy[h, d, s] = cp
            pending.append(cp)
            n_y += 1

    for cp in ab_last:
        cp.wait_recv()
    get_p.wait()

    lane32 = iota((16, 256), 1) >> 5

    def pick_step(b, carry):
        dst = pl.ds(pl.multiple_of(b * 16, 16), 16)
        send_a[dst, :] = aball[where[0, f * 64 + b]]
        v = aball[where[1, f * 64 + b]]
        vb[dst, :] = jnp.where(lane32 == where[2, f * 64 + b], v.astype(F32), 0.0).astype(BF)
        return carry

    lax.fori_loop(0, 64, pick_step, 0)
    el = iota((256, 128), 0)
    ej = iota((256, 128), 1)
    spread = pick(((el & 31) == (ej & 31)) & ((ej >> 5) == (t & 3)))
    send_b[...] = mm(vb[...], spread).astype(BF)

    def my_cols(i, n):
        return pl.ds(pl.multiple_of(i * n, n), n)

    def swap_a(d):
        to = lax.rem(t + d, 32)
        return (
            remote(send_a.at[my_cols(to, 32), :], at.at[:, my_cols(t, 256)], pa_sem, d, (f, to)),
            remote(send_b.at[my_cols(to, 32), :], recv_b.at[t], pb_sem, d, (f, to)),
        )

    def swap_start(d, carry):
        for cp in swap_a(d):
            cp.start()
        return carry

    def swap_recv(d, carry):
        for cp in swap_a(d):
            cp.wait_recv()
        return carry

    def swap_sent(d, carry):
        for cp in swap_a(d):
            cp.wait_send()
        return carry

    lax.fori_loop(1, 32, swap_start, 0)
    at[:, my_cols(t, 256)] = send_a[my_cols(t, 32), :]
    recv_b[t] = send_b[my_cols(t, 32), :]

    wx = {}
    counters = {"x": 0, "c": 0}
    wc = {}
    foreign = (up(f, 3), up(f, 1), up(f, 2))

    def to_sibling(fi, r0, key):
        cp = remote(wslice(fi, r0), wslice(fi, r0), wc_sem, counters["c"], sibling)
        counters["c"] += 1
        cp.start()
        wc[key] = cp
        pending.append(cp)

    def to_plane(fi, r0, d, key, h):
        cp = remote(
            wslice(fi, r0), wslice(fi, r0), wx_sem, counters["x"], (dev_x if h == 0 else dev_z)(d)
        )
        counters["x"] += 1
        cp.start()
        wx[key] = cp
        pending.append(cp)

    fw = {}
    for h in range(2):
        for d, s in ((1, 0), (3, 1)):
            wy[h, d, s].wait_recv()
            src = up(f, 4 - d)
            r0 = base[h] + s * 256
            cp = remote(wslice(src, r0), wslice(src, r0), wy_sem, n_y, dev_y(d))
            n_y += 1
            cp.start()
            fw[h, s] = cp
            pending.append(cp)
        for d, s in ((1, 0), (3, 1), (1, 1), (3, 0)):
            if (d, s) in ((1, 1), (3, 0)):
                wy[h, d, s].wait_recv()
            fi = 0 if d == 1 else 1
            r0 = base[h] + s * 256
            for dd in (1, 3) if s == 0 else (3, 1):
                to_plane(foreign[fi], r0, dd, (h, dd, fi, s), h)
            to_sibling(foreign[fi], r0, (h, 0, fi, s))

    lax.fori_loop(1, 32, swap_recv, 0)
    for q in range(8):
        total = recv_b[4 * q]
        for i in range(1, 4):
            total = total + recv_b[4 * q + i]
        bt[:, q * 128 : (q + 1) * 128] = total

    def rank_step(k, total):
        cols = my_cols(k, 1024)
        return total + mm(xv[:, cols], at[:, cols], NT)

    diagonal = (iota((256, 32), 0) >> 7) == (iota((256, 32), 1) >> 4)
    rank_in = lax.fori_loop(0, 8, rank_step, jnp.zeros((256, 32), F32))
    rank_in = jnp.where(diagonal, rank_in, 0.0).astype(BF)
    rank_grad = jnp.zeros((256, 32), F32)
    for j in range(4):
        rank_grad = rank_grad + mm(go[j], bt[:, j * 256 : (j + 1) * 256], NT)
    rank_grad = jnp.where(diagonal, SCALE * rank_grad, 0.0).astype(BF)
    rg_s[...] = rank_grad

    def terms_step(k, carry):
        cols = my_cols(k, 1024)
        gs[:, cols] = mm(rg_s[...], xv[:, cols], TN).astype(BF)
        return carry

    lax.fori_loop(0, 8, terms_step, 0)
    for j in range(4):
        us[:, j * 256 : (j + 1) * 256] = (SCALE * mm(rank_in, go[j], TN)).astype(BF)

    def swap_g(d):
        to = lax.rem(t + d, 32)
        return (
            remote(gs.at[:, my_cols(to, 256)], terms.at[f, my_cols(t, 32), :], ga_sem, d, (f, to)),
            remote(us.at[:, my_cols(to // 4, 128)], ur.at[my_cols(t, 32), :], gu_sem, d, (f, to)),
        )

    def g_start(d, carry):
        for cp in swap_g(d):
            cp.start()
        return carry

    def g_recv(d, carry):
        for cp in swap_g(d):
            cp.wait_recv()
        return carry

    def g_sent(d, carry):
        for cp in swap_g(d):
            cp.wait_send()
        return carry

    lax.fori_loop(1, 32, g_start, 0)
    terms[f, my_cols(t, 32), :] = gs[:, my_cols(t, 256)]
    ur[my_cols(t, 32), :] = us[:, my_cols(t // 4, 128)]

    for j in range(4):
        lo[:, j * 256 : (j + 1) * 256] = (
            SCALE * mm(rank_in, bt[:, j * 256 : (j + 1) * 256])
        ).astype(BF)

    for h in range(2):
        for s in range(2):
            fw[h, s].wait_recv()
            r0 = base[h] + s * 256
            for dd in (1, 3) if s == 0 else (3, 1):
                to_plane(foreign[2], r0, dd, (h, dd, 2, s), h)
            to_sibling(foreign[2], r0, (h, 0, 2, s))

    lax.fori_loop(1, 32, g_recv, 0)
    packed = jnp.zeros((128, 256), F32)
    ul = iota((128, 256), 0)
    uj = iota((128, 256), 1)
    for q in range(8):
        e = pick(((ul >> 5) == (t & 3)) & ((uj >> 5) == q) & ((ul & 31) == (uj & 31)))
        packed = packed + mm(ur[q * 128 : (q + 1) * 128, :], e)
    terms[f, 1024:1152, :] = packed.astype(BF)
    g_forward = ring_y(
        lambda s: terms.at[f, pl.ds(s * HALF, HALF)],
        lambda i, s: terms.at[i, pl.ds(s * HALF, HALF)],
        gy_sem,
    )

    def here(h, d):
        if h == 0:
            return up(x, d) * 1024 + c * 512
        return 4096 + up(z, d) * 1024 + c * 512

    for fi in range(3):
        for h in range(2):
            for d, s in ((1, 0), (3, 1)):
                wx[h, d, fi, s].wait_recv()
                r0 = here(h, 4 - d) + s * 256
                to_plane(foreign[fi], r0, d, (h, 2, fi, s), h)
                to_sibling(foreign[fi], r0, (h, d, fi, s))
            for d, s in ((1, 1), (3, 0)):
                wx[h, d, fi, s].wait_recv()
                r0 = here(h, 4 - d) + s * 256
                to_sibling(foreign[fi], r0, (h, d, fi, s))

    def tile(row0):
        cols = pl.ds(pl.multiple_of(row0, 256), 256)
        xk = xv[:, cols]
        total = tga[:, cols] + mm(rg_s[...], at[:, cols])
        for fi in foreign:
            wk = wall[fi, cols, :]
            va[fi] += mm(xk, wk)
            total = total + mm(go[fi], wk, NT)
        tgrad[:, cols] = total.astype(BF)

    def tiles(d):
        def step(i, carry):
            h = i // 4
            pos = jnp.where(h == 0, lax.rem(x + d, 4), lax.rem(z + d, 4))
            tile(h * 4096 + pos * 1024 + (i % 4) * 256)
            return carry

        lax.fori_loop(0, 8, step, 0)

    def await_sibling(d):
        for h in range(2):
            for fi in range(3):
                for s in range(2):
                    wc[h, d, fi, s].wait_recv()

    await_sibling(0)
    tiles(0)

    g_last = g_forward()
    for d in (1, 3):
        await_sibling(d)
        tiles(4 - d)

    for fi in range(3):
        for h in range(2):
            for s in range(2):
                wx[h, 2, fi, s].wait_recv()
                to_sibling(foreign[fi], here(h, 2) + s * 256, (h, 2, fi, s))

    shift = iota((16, 1024), 1) - iota((16, 1024), 0) + f * 1024
    dl = iota((256, 128), 0)
    dj = iota((256, 128), 1)
    acc[...] = jnp.zeros_like(acc)

    def reduce_group(fi):
        def step(q, carry):
            for i in range(8):
                key = tenant[fi * 64 + q * 8 + i] * 16
                onehot[i * 16 : (i + 1) * 16, :] = pick(shift == key)
            unpack = pick((dl == q * 32 + dj) & (dj < 32))
            u = mm(terms[fi, 1024:1152, :], unpack).astype(BF)
            lhs = jnp.concatenate([terms[fi, my_cols(q, 128), :], u], axis=1)
            acc[...] += mm(lhs, onehot[...], TN)
            return carry

        lax.fori_loop(0, 8, step, 0)

    reduce_group(f)
    reduce_group(foreign[0])
    reduce_group(foreign[1])
    for cp in g_last:
        cp.wait_recv()
    reduce_group(foreign[2])
    denom = jnp.maximum(cnt[...], 1.0)
    gdown[...] = acc[0:256, :] / denom
    gup[...] = acc[256:288, :] / denom

    await_sibling(2)
    tiles(2)
    for j in range(4):
        cols = slice(j * 256, (j + 1) * 256)
        values[:, cols] = jnp.where(used, va[j] + lo[:, cols].astype(F32), 0.0).astype(BF)

    lax.fori_loop(1, 32, swap_sent, 0)
    lax.fori_loop(1, 32, g_sent, 0)
    for cp in pending:
        cp.wait_send()


def local(tokens, weight, down, up, cotangent, tenant, fill):
    side = up.reshape(32, 8, 8, 16).transpose(1, 3, 2, 0).reshape(128, 256)
    panel = jnp.concatenate([down.T, side], axis=0)
    owner, slot = tenant // 64, tenant % 64
    where = jnp.stack([owner * 72 + slot, owner * 72 + 64 + slot // 8, slot % 8])
    any_ = pl.BlockSpec(memory_space=pl.ANY)
    vmem = pl.BlockSpec(memory_space=pltpu.VMEM)
    smem = pl.BlockSpec(memory_space=pltpu.SMEM)
    dma = pltpu.SemaphoreType.DMA
    V = pltpu.VMEM
    return pl.pallas_call(
        kernel,
        out_shape=(
            jax.ShapeDtypeStruct((256, 1024), BF),
            jax.ShapeDtypeStruct((256, 8192), BF),
            jax.ShapeDtypeStruct((256, 1024), F32),
            jax.ShapeDtypeStruct((32, 1024), F32),
        ),
        in_specs=[any_, any_, vmem, vmem, smem, smem, smem],
        out_specs=(vmem, vmem, vmem, vmem),
        scratch_shapes=[
            V((256, 8192), BF),
            V((4, 8192, 256), BF),
            V((4, 256, 256), BF),
            V((4, 256, 256), F32),
            V((256, 8192), F32),
            V((288, 16, 256), BF),
            V((1024, 256), BF),
            V((1024, 256), BF),
            V((1024, 128), BF),
            V((32, 8192), BF),
            V((32, 32, 128), BF),
            V((32, 1024), BF),
            V((32, 8192), BF),
            V((32, 1024), BF),
            V((1024, 128), BF),
            V((4, PANEL, 256), BF),
            V((256, 1024), BF),
            V((256, 32), BF),
            V((128, 1024), BF),
            V((384, 1024), F32),
            V((1, 1024), F32),
            dma((3,)),
            dma((2, 6)),
            dma((2, 12)),
            dma((2, 36)),
            dma((2, 48)),
            dma((2, 32)),
            dma((2, 32)),
            dma((2, 32)),
            dma((2, 32)),
            dma((2, 6)),
        ],
        compiler_params=pltpu.CompilerParams(
            has_side_effects=True, vmem_limit_bytes=60 * 1024 * 1024
        ),
        cost_estimate=pl.CostEstimate(
            flops=9_000_000_000, bytes_accessed=30_000_000, transcendentals=0
        ),
    )(tokens, weight, panel.reshape(72, 16, 256), cotangent, tenant, fill, where)


def solution(mesh):
    placed = (
        P(("fsdp", "tok"), None),
        P(None, "fsdp"),
        P("tok", "fsdp"),
        P("tok", "fsdp"),
        P(("fsdp", "tok"), None),
        P(),
        P(),
    )
    return jax.shard_map(
        local,
        mesh=mesh,
        in_specs=placed,
        out_specs=(
            P(("fsdp", "tok"), None),
            P(("fsdp", "tok"), None),
            P("tok", "fsdp"),
            P("tok", "fsdp"),
        ),
        check_vma=False,
    )
```

```python
import jax
import jax.numpy as jnp
from jax import lax
from jax.experimental import pallas as pl
from jax.experimental.pallas import tpu as pltpu
from jax.sharding import PartitionSpec as P

RANK = 16
BLOCK = 128
SCALE = 2.0
BF = jnp.bfloat16
F32 = jnp.float32
NT = (((1,), (1,)), ((), ()))
TN = (((0,), (0,)), ((), ()))


def mm(a, b, dims=(((1,), (0,)), ((), ()))):
    return lax.dot_general(a, b, dims, preferred_element_type=F32)


def iota(shape, dim):
    return lax.broadcasted_iota(jnp.int32, shape, dim)


def pick(cond):
    return jnp.where(cond, 1.0, 0.0).astype(BF)


def kernel(
    x_hbm,
    w_hbm,
    down,
    upmap,
    cot,
    tenant,
    fill,
    where,
    values,
    tgrad,
    gdown,
    gup,
    xv,
    wall,
    go,
    va,
    tga,
    tg_v,
    ab0,
    ab1,
    send_0,
    send_1,
    vb,
    send_b,
    at,
    recv_b,
    bt,
    gs,
    us,
    ur,
    te0,
    te1,
    lo,
    ri_s,
    rg_s,
    onehot,
    acc,
    cnt,
    loc,
    ab_sem,
    wy_sem,
    wx_sem,
    wc_sem,
    p0_sem,
    p1_sem,
    pb_sem,
    g0_sem,
    g1_sem,
    gu_sem,
    gy_sem,
):
    f = lax.axis_index("fsdp")
    t = lax.axis_index("tok")
    x = t // 8
    z = (t // 2) % 4
    c = t % 2

    def up(i, d):
        return lax.rem(i + d, 4)

    def dev_y(d):
        return (up(f, d), t)

    def dev_x(d):
        return (f, up(x, d) * 8 + z * 2 + c)

    def dev_z(d):
        return (f, x * 8 + up(z, d) * 2 + c)

    sibling = (f, x * 8 + z * 2 + (1 - c))

    def remote(src, dst, sem, i, dev):
        return pltpu.make_async_remote_copy(
            src_ref=src,
            dst_ref=dst,
            send_sem=sem.at[0, i],
            recv_sem=sem.at[1, i],
            device_id=dev,
            device_id_type=pl.DeviceIdType.MESH,
        )

    def my_cols(i, n):
        return pl.ds(pl.multiple_of(i * n, n), n)

    barrier = pltpu.get_barrier_semaphore()
    for d in (1, 3):
        pl.semaphore_signal(
            barrier, inc=1, device_id=dev_y(d), device_id_type=pl.DeviceIdType.MESH
        )

    def greet(d, carry):
        pl.semaphore_signal(
            barrier,
            inc=1,
            device_id=(f, lax.rem(t + d, 32)),
            device_id_type=pl.DeviceIdType.MESH,
        )
        return carry

    lax.fori_loop(1, 32, greet, 0)

    get_x = pltpu.make_async_copy(x_hbm, xv, loc.at[0])
    get_w = pltpu.make_async_copy(w_hbm, wall.at[f], loc.at[1])
    get_x.start()
    get_w.start()

    ab0[pl.ds(f * 80, 64)] = down[0:128, :].astype(F32).T.astype(BF).reshape(64, 16, 128)
    ab1[pl.ds(f * 64, 64)] = down[128:256, :].astype(F32).T.astype(BF).reshape(64, 16, 128)
    side = jnp.zeros((16, 16, 128), F32)
    for g in range(4):
        place = pick(iota((32, 128), 1) == iota((32, 128), 0) + 32 * g)
        moved = mm(upmap[...], place, TN).reshape(16, 64, 128)
        side = side + moved[:, g * 16 : (g + 1) * 16, :]
    ab0[pl.ds(f * 80 + 64, 16)] = side.astype(BF)

    pl.semaphore_wait(barrier, 33)

    pending = []

    def ring_y(part_of, sem, n0):
        first = {}
        last = []

        def start():
            for i, (d, s) in enumerate(((1, 0), (3, 1), (1, 1), (3, 0))):
                cp = remote(part_of(f, s), part_of(f, s), sem, n0 + i, dev_y(d))
                cp.start()
                first[d, s] = cp
                pending.append(cp)

        def forward():
            for i, (d, s) in enumerate(((1, 0), (3, 1))):
                first[d, s].wait_recv()
                src = up(f, 4 - d)
                cp = remote(
                    part_of(src, s), part_of(src, s), sem, n0 + 4 + i, dev_y(d)
                )
                cp.start()
                last.append(cp)
                pending.append(cp)

        def near():
            first[1, 1].wait_recv()
            first[3, 0].wait_recv()

        def far():
            for cp in last:
                cp.wait_recv()

        return start, forward, near, far

    p_start, p_forward, p_near, p_far = ring_y(
        lambda i, s: ab0.at[pl.ds(i * 80 + s * 40, 40)], ab_sem, 0
    )
    q_start, q_forward, q_near, q_far = ring_y(
        lambda i, s: ab1.at[pl.ds(i * 64 + s * 32, 32)], ab_sem, 6
    )
    p_start()

    b0 = (f * 32 + t) * 2

    def used_rows():
        rows = iota((256, 1), 0)
        return rows < jnp.where(rows < BLOCK, fill[b0], fill[b0 + 1] + BLOCK)

    used = used_rows()
    for j in range(4):
        go[j] = jnp.where(used, cot[:, j * 256 : (j + 1) * 256].astype(F32), 0.0).astype(BF)
    va[...] = jnp.zeros_like(va)
    get_x.wait()
    get_w.wait()

    def own_step(k, carry):
        cols = my_cols(k, 256)
        wk = wall[f, cols, :]
        va[f] += mm(xv[:, cols], wk)
        tga[:, cols] = mm(go[f], wk, NT)
        return carry

    p_forward()
    q_start()
    lax.fori_loop(0, 12, own_step, 0)
    p_near()
    p_far()

    lane32 = iota((16, 128), 1) >> 5

    def pick_0(b, carry):
        dst = my_cols(b, 16)
        send_0[dst, :] = ab0[where[0, f * 64 + b]]
        v = ab0[where[1, f * 64 + b]]
        vb[dst, :] = jnp.where(lane32 == where[2, f * 64 + b], v.astype(F32), 0.0).astype(BF)
        return carry

    def pick_1(b, carry):
        send_1[my_cols(b, 16), :] = ab1[where[3, f * 64 + b]]
        return carry

    el = iota((128, 128), 0)
    ej = iota((128, 128), 1)

    def swap_0(d):
        to = lax.rem(t + d, 32)
        return (
            remote(send_0.at[my_cols(to, 32), :], at.at[:, my_cols(t * 2, 128)], p0_sem, d, (f, to)),
            remote(send_b.at[my_cols(to, 32), :], recv_b.at[t], pb_sem, d, (f, to)),
        )

    def swap_1(d):
        to = lax.rem(t + d, 32)
        return (
            remote(
                send_1.at[my_cols(to, 32), :], at.at[:, my_cols(t * 2 + 1, 128)], p1_sem, d, (f, to)
            ),
        )

    def over_tok(copies, act):
        def step(d, carry):
            for cp in copies(d):
                if act == "start":
                    cp.start()
                elif act == "recv":
                    cp.wait_recv()
                else:
                    cp.wait_send()
            return carry

        lax.fori_loop(1, 32, step, 0)

    lax.fori_loop(0, 64, pick_0, 0)
    spread = pick(((el & 31) == (ej & 31)) & ((ej >> 5) == (t & 3)))
    send_b[...] = mm(vb[...], spread).astype(BF)
    over_tok(swap_0, "start")
    q_forward()

    base = (x * 1024 + c * 512, 4096 + z * 1024 + c * 512)

    def wslice(fi, row0):
        return wall.at[fi, pl.ds(pl.multiple_of(row0, 256), 256), :]

    wy = {}
    n_y = 0
    for h in range(2):
        for d, s in ((1, 0), (3, 1), (1, 1), (3, 0)):
            r0 = base[h] + s * 256
            cp = remote(
                w_hbm.at[pl.ds(pl.multiple_of(r0, 256), 256), :],
                wslice(f, r0),
                wy_sem,
                n_y,
                dev_y(d),
            )
            cp.start()
            wy[h, d, s] = cp
            pending.append(cp)
            n_y += 1

    at[:, my_cols(t * 2, 128)] = send_0[my_cols(t, 32), :]
    recv_b[t] = send_b[my_cols(t, 32), :]
    q_near()
    q_far()
    lax.fori_loop(0, 64, pick_1, 0)
    over_tok(swap_1, "start")
    at[:, my_cols(t * 2 + 1, 128)] = send_1[my_cols(t, 32), :]

    lax.fori_loop(12, 32, own_step, 0)

    wx = {}
    counters = {"x": 0, "c": 0}
    wc = {}
    foreign = (up(f, 3), up(f, 1), up(f, 2))

    def to_sibling(fi, r0, key):
        cp = remote(wslice(fi, r0), wslice(fi, r0), wc_sem, counters["c"], sibling)
        counters["c"] += 1
        cp.start()
        wc[key] = cp
        pending.append(cp)

    def to_plane(fi, r0, d, key, h):
        cp = remote(
            wslice(fi, r0), wslice(fi, r0), wx_sem, counters["x"], (dev_x if h == 0 else dev_z)(d)
        )
        counters["x"] += 1
        cp.start()
        wx[key] = cp
        pending.append(cp)

    fw = {}

    def w_near(h):
        nonlocal n_y
        for d, s in ((1, 0), (3, 1)):
            wy[h, d, s].wait_recv()
            src = up(f, 4 - d)
            r0 = base[h] + s * 256
            cp = remote(wslice(src, r0), wslice(src, r0), wy_sem, n_y, dev_y(d))
            n_y += 1
            cp.start()
            fw[h, s] = cp
            pending.append(cp)
        for d, s in ((1, 0), (3, 1), (1, 1), (3, 0)):
            if (d, s) in ((1, 1), (3, 0)):
                wy[h, d, s].wait_recv()
            fi = 0 if d == 1 else 1
            r0 = base[h] + s * 256
            for dd in (1, 3) if s == 0 else (3, 1):
                to_plane(foreign[fi], r0, dd, (h, dd, fi, s), h)
            to_sibling(foreign[fi], r0, (h, 0, fi, s))

    def w_far(h):
        for s in range(2):
            fw[h, s].wait_recv()
            r0 = base[h] + s * 256
            for dd in (1, 3) if s == 0 else (3, 1):
                to_plane(foreign[2], r0, dd, (h, dd, 2, s), h)
            to_sibling(foreign[2], r0, (h, 0, 2, s))

    def here(h, d):
        if h == 0:
            return up(x, d) * 1024 + c * 512
        return 4096 + up(z, d) * 1024 + c * 512

    def w_along(h, fi):
        for d, s in ((1, 0), (3, 1)):
            wx[h, d, fi, s].wait_recv()
            r0 = here(h, 4 - d) + s * 256
            to_plane(foreign[fi], r0, d, (h, 2, fi, s), h)
            to_sibling(foreign[fi], r0, (h, d, fi, s))
        for d, s in ((1, 1), (3, 0)):
            wx[h, d, fi, s].wait_recv()
            r0 = here(h, 4 - d) + s * 256
            to_sibling(foreign[fi], r0, (h, d, fi, s))

    w_near(0)

    tlane = (iota((1, 1024), 1) >> 4) + f * 64

    def count_step(b, total):
        return total + jnp.where(tlane == tenant[b], fill[b].astype(F32), 0.0)

    cnt[...] = lax.fori_loop(0, 256, count_step, jnp.zeros((1, 1024), F32))

    over_tok(swap_0, "recv")
    for q in range(8):
        total = recv_b[4 * q]
        for i in range(1, 4):
            total = total + recv_b[4 * q + i]
        bt[:, q * 128 : (q + 1) * 128] = total
    diagonal = (iota((256, 32), 0) >> 7) == (iota((256, 32), 1) >> 4)
    rank_grad = jnp.zeros((256, 32), F32)
    for j in range(4):
        rank_grad = rank_grad + mm(go[j], bt[:, j * 256 : (j + 1) * 256], NT)
    rg_s[...] = jnp.where(diagonal, SCALE * rank_grad, 0.0).astype(BF)

    def terms_step(k, carry):
        cols = my_cols(k, 1024)
        gs[:, cols] = mm(rg_s[...], xv[:, cols], TN).astype(BF)
        return carry

    lax.fori_loop(0, 8, terms_step, 0)

    def back_0(d):
        to = lax.rem(t + d, 32)
        return (
            remote(gs.at[:, my_cols(to * 2, 128)], te0.at[f, my_cols(t, 32), :], g0_sem, d, (f, to)),
        )

    def back_1(d):
        to = lax.rem(t + d, 32)
        return (
            remote(
                gs.at[:, my_cols(to * 2 + 1, 128)], te1.at[f, my_cols(t, 32), :], g1_sem, d, (f, to)
            ),
            remote(us.at[:, my_cols(to // 4, 128)], ur.at[my_cols(t, 32), :], gu_sem, d, (f, to)),
        )

    over_tok(back_0, "start")
    te0[f, my_cols(t, 32), :] = gs[:, my_cols(t * 2, 128)]

    over_tok(swap_1, "recv")

    def rank_step(k, total):
        cols = my_cols(k, 1024)
        return total + mm(xv[:, cols], at[:, cols], NT)

    rank_in = lax.fori_loop(0, 8, rank_step, jnp.zeros((256, 32), F32))
    ri_s[...] = jnp.where(diagonal, rank_in, 0.0).astype(BF)
    for j in range(4):
        us[:, j * 256 : (j + 1) * 256] = (SCALE * mm(ri_s[...], go[j], TN)).astype(BF)
    over_tok(back_1, "start")
    te1[f, my_cols(t, 32), :] = gs[:, my_cols(t * 2 + 1, 128)]
    ur[my_cols(t, 32), :] = us[:, my_cols(t // 4, 128)]

    w_near(1)
    w_far(0)

    u_start, u_forward, u_near, u_far = ring_y(
        lambda i, s: te0.at[i, pl.ds(s * 512, 512)], gy_sem, 0
    )
    v_start, v_forward, v_near, v_far = ring_y(
        lambda i, s: te1.at[i, pl.ds(s * 640, 640)], gy_sem, 6
    )
    over_tok(back_0, "recv")
    u_start()

    w_far(1)
    for h in range(2):
        w_along(h, 0)

    over_tok(back_1, "recv")
    packed = jnp.zeros((256, 128), F32)
    for q in range(4):
        e = pick(((el >> 5) == (t & 3)) & ((ej >> 5) == q) & ((el & 31) == (ej & 31)))
        packed = packed + mm(ur[q * 256 : (q + 1) * 256, :], e)
    te1[f, 1024:1280, :] = packed.astype(BF)
    u_forward()
    v_start()

    for h in range(2):
        w_along(h, 1)

    for j in range(4):
        lo[:, j * 256 : (j + 1) * 256] = (
            SCALE * mm(ri_s[...], bt[:, j * 256 : (j + 1) * 256])
        ).astype(BF)

    def tile(row0):
        cols = pl.ds(pl.multiple_of(row0, 256), 256)
        xk = xv[:, cols]
        total = tga[:, cols] + mm(rg_s[...], at[:, cols])
        for fi in foreign:
            wk = wall[fi, cols, :]
            va[fi] += mm(xk, wk)
            total = total + mm(go[fi], wk, NT)
        tg_v[:, cols] = total.astype(BF)
        pltpu.make_async_copy(tg_v.at[:, cols], tgrad.at[:, cols], loc.at[2]).start()

    def tiles(d):
        def step(i, carry):
            h = i // 4
            pos = jnp.where(h == 0, lax.rem(x + d, 4), lax.rem(z + d, 4))
            tile(h * 4096 + pos * 1024 + (i % 4) * 256)
            return carry

        lax.fori_loop(0, 8, step, 0)

    def await_sibling(d):
        for h in range(2):
            for fi in range(3):
                for s in range(2):
                    wc[h, d, fi, s].wait_recv()

    await_sibling(0)
    tiles(0)
    u_near()
    v_forward()
    for h in range(2):
        w_along(h, 2)

    shift = iota((16, 1024), 1) - iota((16, 1024), 0) + f * 1024
    acc[...] = jnp.zeros_like(acc)

    def reduce_group(fi):
        def step(q, carry):
            for i in range(8):
                key = tenant[fi * 64 + q * 8 + i] * 16
                onehot[i * 16 : (i + 1) * 16, :] = pick(shift == key)
            unpack = pick((el == (q // 2) * 32 + ej) & (ej < 32))
            u = mm(te1[fi, my_cols(8 + q % 2, 128), :], unpack).astype(BF)
            lhs = jnp.concatenate(
                [te0[fi, my_cols(q, 128), :], te1[fi, my_cols(q, 128), :], u], axis=1
            )
            acc[...] += mm(lhs, onehot[...], TN)
            return carry

        lax.fori_loop(0, 8, step, 0)

    reduce_group(f)
    await_sibling(1)
    tiles(3)
    await_sibling(3)
    tiles(1)
    for fi in range(3):
        for h in range(2):
            for s in range(2):
                wx[h, 2, fi, s].wait_recv()
                to_sibling(foreign[fi], here(h, 2) + s * 256, (h, 2, fi, s))
    v_near()
    reduce_group(foreign[0])
    reduce_group(foreign[1])
    await_sibling(2)
    tiles(2)
    used = used_rows()
    for j in range(4):
        cols = slice(j * 256, (j + 1) * 256)
        values[:, cols] = jnp.where(used, va[j] + lo[:, cols].astype(F32), 0.0).astype(BF)
    u_far()
    v_far()
    reduce_group(foreign[2])
    denom = jnp.maximum(cnt[...], 1.0)
    gdown[...] = acc[0:256, :] / denom
    gup[...] = acc[256:288, :] / denom

    pltpu.make_async_copy(tg_v, tgrad, loc.at[2]).wait()
    for copies in (swap_0, swap_1, back_0, back_1):
        over_tok(copies, "sent")
    for cp in pending:
        cp.wait_send()


def hand_on(v_in, t_in, d_in, u_in, v_out, t_out, d_out, u_out, sem):
    copies = [(v_in, v_out), (d_in, d_out), (u_in, u_out)]
    for i in range(8):
        rows = pl.ds(i * 32, 32)
        copies.append((t_in.at[rows, :], t_out.at[rows, :]))
    copies = [
        pltpu.make_async_copy(a, b, sem.at[i]) for i, (a, b) in enumerate(copies)
    ]
    for cp in copies:
        cp.start()
    for cp in copies:
        cp.wait()


def local(tokens, weight, down, up, cotangent, tenant, fill):
    owner, slot = tenant // 64, tenant % 64
    where = jnp.stack(
        [owner * 80 + slot, owner * 80 + 64 + slot // 4, slot % 4, owner * 64 + slot]
    )
    any_ = pl.BlockSpec(memory_space=pl.ANY)
    vmem = pl.BlockSpec(memory_space=pltpu.VMEM)
    smem = pl.BlockSpec(memory_space=pltpu.SMEM)
    dma = pltpu.SemaphoreType.DMA
    V = pltpu.VMEM
    out_shape = (
        jax.ShapeDtypeStruct((256, 1024), BF),
        jax.ShapeDtypeStruct((256, 8192), BF),
        jax.ShapeDtypeStruct((256, 1024), F32),
        jax.ShapeDtypeStruct((32, 1024), F32),
    )
    outs = pl.pallas_call(
        kernel,
        out_shape=out_shape,
        in_specs=[any_, any_, vmem, vmem, vmem, smem, smem, smem],
        out_specs=(vmem, any_, vmem, vmem),
        scratch_shapes=[
            V((256, 8192), BF),
            V((4, 8192, 256), BF),
            V((4, 256, 256), BF),
            V((4, 256, 256), F32),
            V((256, 8192), F32),
            V((256, 8192), BF),
            V((320, 16, 128), BF),
            V((256, 16, 128), BF),
            V((1024, 128), BF),
            V((1024, 128), BF),
            V((1024, 128), BF),
            V((1024, 128), BF),
            V((32, 8192), BF),
            V((32, 32, 128), BF),
            V((32, 1024), BF),
            V((32, 8192), BF),
            V((32, 1024), BF),
            V((1024, 128), BF),
            V((4, 1024, 128), BF),
            V((4, 1280, 128), BF),
            V((256, 1024), BF),
            V((256, 32), BF),
            V((256, 32), BF),
            V((128, 1024), BF),
            V((384, 1024), F32),
            V((1, 1024), F32),
            dma((3,)),
            dma((2, 12)),
            dma((2, 12)),
            dma((2, 36)),
            dma((2, 48)),
            dma((2, 32)),
            dma((2, 32)),
            dma((2, 32)),
            dma((2, 32)),
            dma((2, 32)),
            dma((2, 32)),
            dma((2, 12)),
        ],
        compiler_params=pltpu.CompilerParams(
            has_side_effects=True, collective_id=1, vmem_limit_bytes=60 * 1024 * 1024
        ),
        cost_estimate=pl.CostEstimate(
            flops=9_000_000_000, bytes_accessed=30_000_000, transcendentals=0
        ),
    )(tokens, weight, down, up, cotangent, tenant, fill, where)
    return pl.pallas_call(
        hand_on,
        out_shape=out_shape,
        in_specs=[any_] * 4,
        out_specs=(any_,) * 4,
        scratch_shapes=[dma((11,))],
    )(*outs)


def solution(mesh):
    placed = (
        P(("fsdp", "tok"), None),
        P(None, "fsdp"),
        P("tok", "fsdp"),
        P("tok", "fsdp"),
        P(("fsdp", "tok"), None),
        P(),
        P(),
    )
    return jax.shard_map(
        local,
        mesh=mesh,
        in_specs=placed,
        out_specs=(
            P(("fsdp", "tok"), None),
            P(("fsdp", "tok"), None),
            P("tok", "fsdp"),
            P("tok", "fsdp"),
        ),
        check_vma=False,
    )
```

```python
import jax
import jax.numpy as jnp
from jax import lax
from jax.experimental import pallas as pl
from jax.experimental.pallas import tpu as pltpu
from jax.sharding import PartitionSpec as P

RANK = 16
BLOCK = 128
SCALE = 2.0
BF = jnp.bfloat16
F32 = jnp.float32
NT = (((1,), (1,)), ((), ()))
TN = (((0,), (0,)), ((), ()))


def mm(a, b, dims=(((1,), (0,)), ((), ()))):
    return lax.dot_general(a, b, dims, preferred_element_type=F32)


def iota(shape, dim):
    return lax.broadcasted_iota(jnp.int32, shape, dim)


def pick(cond):
    return jnp.where(cond, 1.0, 0.0).astype(BF)


def kernel(
    x_hbm,
    w_hbm,
    down,
    upmap,
    cot,
    tenant,
    fill,
    where,
    values,
    tgrad,
    te_out,
    tu_out,
    xv,
    wall,
    go,
    va,
    tga,
    tg_v,
    ab_a,
    ab_b,
    send_a,
    vb,
    send_b,
    at,
    recv_b,
    bt,
    gs,
    us,
    ur,
    te,
    tu,
    lo,
    ri_s,
    rg_s,
    loc,
    y_sem,
    wy_sem,
    wl_sem,
    wx_sem,
    wc_sem,
    pa_sem,
    pb_sem,
    gt_sem,
    gu_sem,
):
    f = lax.axis_index("fsdp")
    t = lax.axis_index("tok")
    x = t // 8
    z = (t // 2) % 4
    c = t % 2

    def up(i, d):
        return lax.rem(i + d, 4)

    def dev_y(d):
        return (up(f, d), t)

    def dev_x(d):
        return (f, up(x, d) * 8 + z * 2 + c)

    def dev_z(d):
        return (f, x * 8 + up(z, d) * 2 + c)

    sibling = (f, x * 8 + z * 2 + (1 - c))

    def remote(src, dst, sem, i, dev):
        return pltpu.make_async_remote_copy(
            src_ref=src,
            dst_ref=dst,
            send_sem=sem.at[0, i],
            recv_sem=sem.at[1, i],
            device_id=dev,
            device_id_type=pl.DeviceIdType.MESH,
        )

    def my_cols(i, n):
        return pl.ds(pl.multiple_of(i * n, n), n)

    barrier = pltpu.get_barrier_semaphore()
    for d in (1, 3):
        pl.semaphore_signal(
            barrier, inc=1, device_id=dev_y(d), device_id_type=pl.DeviceIdType.MESH
        )

    def greet(d, carry):
        pl.semaphore_signal(
            barrier,
            inc=1,
            device_id=(f, lax.rem(t + d, 32)),
            device_id_type=pl.DeviceIdType.MESH,
        )
        return carry

    lax.fori_loop(1, 32, greet, 0)

    get_x = pltpu.make_async_copy(x_hbm, xv, loc.at[0])
    get_w = pltpu.make_async_copy(w_hbm, wall.at[f], loc.at[1])
    get_x.start()
    get_w.start()

    side = jnp.zeros((16, 16, 128), F32)
    for g in range(4):
        place = pick(iota((32, 128), 1) == iota((32, 128), 0) + 32 * g)
        moved = mm(upmap[...], place, TN).reshape(16, 64, 128)
        side = side + moved[:, g * 16 : (g + 1) * 16, :]
    ab_b[pl.ds(f * 16, 16)] = side.astype(BF)
    ab_a[pl.ds(f * 64, 64)] = down[...].astype(F32).T.astype(BF).reshape(64, 16, 256)

    pl.semaphore_wait(barrier, 33)

    pending = []

    def ring_y(part_of, sem, n0):
        first = {}
        last = []

        def start():
            for i, (d, s) in enumerate(((1, 0), (3, 1), (1, 1), (3, 0))):
                cp = remote(part_of(f, s), part_of(f, s), sem, n0 + i, dev_y(d))
                cp.start()
                first[d, s] = cp
                pending.append(cp)

        def forward():
            for i, (d, s) in enumerate(((1, 0), (3, 1))):
                first[d, s].wait_recv()
                src = up(f, 4 - d)
                cp = remote(
                    part_of(src, s), part_of(src, s), sem, n0 + 4 + i, dev_y(d)
                )
                cp.start()
                last.append(cp)
                pending.append(cp)

        def near():
            first[1, 1].wait_recv()
            first[3, 0].wait_recv()

        def far():
            for cp in last:
                cp.wait_recv()

        return start, forward, near, far

    b_start, b_forward, b_near, b_far = ring_y(
        lambda i, s: ab_b.at[pl.ds(i * 16 + s * 8, 8)], y_sem, 0
    )
    a_start, a_forward, a_near, a_far = ring_y(
        lambda i, s: ab_a.at[pl.ds(i * 64 + s * 32, 32)], y_sem, 6
    )
    t_start, t_forward, t_near, t_far = ring_y(
        lambda i, s: te.at[i, pl.ds(s * 512, 512)], y_sem, 12
    )
    u_start, u_forward, u_near, u_far = ring_y(
        lambda i, s: tu.at[i, pl.ds(s * 128, 128)], y_sem, 18
    )
    b_start()

    base = (x * 1024 + c * 512, 4096 + z * 1024 + c * 512)
    pos1 = (z, x)
    dev1 = (dev_z, dev_x)
    dev2 = (dev_x, dev_z)

    def wslice(fi, row0, n):
        return wall.at[fi, pl.ds(pl.multiple_of(row0, 64), n), :]

    def sub_at(h, d):
        return base[h] + up(pos1[h], d) * 128

    wy = {}
    n_y = 0
    for h in range(2):
        for d, s in ((1, 0), (3, 1), (1, 1), (3, 0)):
            r0 = sub_at(h, 0) + s * 64
            cp = remote(
                w_hbm.at[pl.ds(pl.multiple_of(r0, 64), 64), :],
                wslice(f, r0, 64),
                wy_sem,
                n_y,
                dev_y(d),
            )
            cp.start()
            wy[h, d, s] = cp
            pending.append(cp)
            n_y += 1
    a_start()

    b0 = (f * 32 + t) * 2

    def used_rows():
        rows = iota((256, 1), 0)
        return rows < jnp.where(rows < BLOCK, fill[b0], fill[b0 + 1] + BLOCK)

    used = used_rows()
    for j in range(4):
        go[j] = jnp.where(used, cot[:, j * 256 : (j + 1) * 256].astype(F32), 0.0).astype(BF)

    b_forward()
    va[...] = jnp.zeros_like(va)
    b_near()

    wl = {}
    wx = {}
    wc = {}
    fw = {}
    counters = {"l": 0, "x": 0, "c": 0}
    foreign = (up(f, 3), up(f, 1), up(f, 2))

    def same_place(fi, r0, n, sem, kind, dev):
        cp = remote(wslice(fi, r0, n), wslice(fi, r0, n), sem, counters[kind], dev)
        counters[kind] += 1
        cp.start()
        pending.append(cp)
        return cp

    def to_sibling(fi, r0, key):
        wc[key] = same_place(fi, r0, 256, wc_sem, "c", sibling)

    def w_near(h):
        nonlocal n_y
        for d, s in ((1, 0), (3, 1)):
            wy[h, d, s].wait_recv()
            src = up(f, 4 - d)
            r0 = sub_at(h, 0) + s * 64
            cp = remote(wslice(src, r0, 64), wslice(src, r0, 64), wy_sem, n_y, dev_y(d))
            n_y += 1
            cp.start()
            fw[h, s] = cp
            pending.append(cp)
        for d, s in ((1, 1), (3, 0)):
            wy[h, d, s].wait_recv()
        for fi in range(2):
            for dd in (1, 3):
                wl[h, dd, fi] = same_place(
                    foreign[fi], sub_at(h, 0), 128, wl_sem, "l", dev1[h](dd)
                )

    def w_far(h):
        for s in range(2):
            fw[h, s].wait_recv()
        for dd in (1, 3):
            wl[h, dd, 2] = same_place(
                foreign[2], sub_at(h, 0), 128, wl_sem, "l", dev1[h](dd)
            )

    def w_line(h, fi):
        for d, s in ((1, 0), (3, 1)):
            wl[h, d, fi].wait_recv()
            wl[h, 2, fi, s] = same_place(
                foreign[fi], sub_at(h, 4 - d) + s * 64, 64, wl_sem, "l", dev1[h](d)
            )

    def to_plane(fi, r0, d, key, h):
        wx[key] = same_place(fi, r0, 256, wx_sem, "x", dev2[h](d))

    def w_plane(h, fi):
        for s in range(2):
            wl[h, 2, fi, s].wait_recv()
        for s in range(2):
            r0 = base[h] + s * 256
            for dd in (1, 3) if s == 0 else (3, 1):
                to_plane(foreign[fi], r0, dd, (h, dd, fi, s), h)
        for s in range(2):
            to_sibling(foreign[fi], base[h] + s * 256, (h, 0, fi, s))

    def here(h, d):
        if h == 0:
            return up(x, d) * 1024 + c * 512
        return 4096 + up(z, d) * 1024 + c * 512

    def w_along(h, fi):
        for d, s in ((1, 0), (3, 1)):
            wx[h, d, fi, s].wait_recv()
            r0 = here(h, 4 - d) + s * 256
            to_plane(foreign[fi], r0, d, (h, 2, fi, s), h)
            to_sibling(foreign[fi], r0, (h, d, fi, s))
        for d, s in ((1, 1), (3, 0)):
            wx[h, d, fi, s].wait_recv()
            r0 = here(h, 4 - d) + s * 256
            to_sibling(foreign[fi], r0, (h, d, fi, s))

    b_far()

    lane32 = iota((16, 128), 1) >> 5
    el = iota((128, 128), 0)
    ej = iota((128, 128), 1)

    def pick_b(b, carry):
        v = ab_b[where[0, f * 64 + b]]
        vb[my_cols(b, 16), :] = jnp.where(
            lane32 == where[1, f * 64 + b], v.astype(F32), 0.0
        ).astype(BF)
        return carry

    def pick_a(b, carry):
        send_a[my_cols(b, 16), :] = ab_a[tenant[f * 64 + b]]
        return carry

    def swap_a(d):
        to = lax.rem(t + d, 32)
        return remote(
            send_a.at[my_cols(to, 32), :], at.at[:, my_cols(t, 256)], pa_sem, d, (f, to)
        )

    def swap_b(d):
        to = lax.rem(t + d, 32)
        return remote(send_b.at[my_cols(to, 32), :], recv_b.at[t], pb_sem, d, (f, to))

    def back_t(d):
        to = lax.rem(t + d, 32)
        return remote(
            gs.at[:, my_cols(to, 256)], te.at[f, my_cols(t, 32), :], gt_sem, d, (f, to)
        )

    def back_u(d):
        to = lax.rem(t + d, 32)
        return remote(
            us.at[:, my_cols(to // 4, 128)], ur.at[my_cols(t, 32), :], gu_sem, d, (f, to)
        )

    def over_tok(copy, act):
        def step(d, carry):
            cp = copy(d)
            if act == "start":
                cp.start()
            elif act == "recv":
                cp.wait_recv()
            else:
                cp.wait_send()
            return carry

        lax.fori_loop(1, 32, step, 0)

    lax.fori_loop(0, 64, pick_b, 0)
    spread = pick(((el & 31) == (ej & 31)) & ((ej >> 5) == (t & 3)))
    send_b[...] = mm(vb[...], spread).astype(BF)
    over_tok(swap_b, "start")
    recv_b[t] = send_b[my_cols(t, 32), :]

    get_x.wait()
    w_near(0)
    w_near(1)

    over_tok(swap_b, "recv")
    for q in range(8):
        total = recv_b[4 * q]
        for i in range(1, 4):
            total = total + recv_b[4 * q + i]
        bt[:, q * 128 : (q + 1) * 128] = total
    diagonal = (iota((256, 32), 0) >> 7) == (iota((256, 32), 1) >> 4)
    rank_grad = jnp.zeros((256, 32), F32)
    for j in range(4):
        rank_grad = rank_grad + mm(go[j], bt[:, j * 256 : (j + 1) * 256], NT)
    rg_s[...] = jnp.where(diagonal, SCALE * rank_grad, 0.0).astype(BF)

    def terms_step(k, carry):
        cols = my_cols(k, 1024)
        gs[:, cols] = mm(rg_s[...], xv[:, cols], TN).astype(BF)
        return carry

    lax.fori_loop(0, 8, terms_step, 0)
    over_tok(back_t, "start")
    te[f, my_cols(t, 32), :] = gs[:, my_cols(t, 256)]

    w_far(0)
    w_far(1)
    for h in range(2):
        w_line(h, 0)
        w_line(h, 1)
    a_forward()
    get_w.wait()

    def own_step(k, carry):
        cols = my_cols(k, 256)
        wk = wall[f, cols, :]
        va[f] += mm(xv[:, cols], wk)
        tga[:, cols] = mm(go[f], wk, NT)
        return carry

    lax.fori_loop(0, 8, own_step, 0)
    for h in range(2):
        w_line(h, 2)
    for fi in range(2):
        for h in range(2):
            w_plane(h, fi)
    over_tok(back_t, "recv")
    t_start()
    put_own = pltpu.make_async_copy(te.at[f], te_out.at[f], loc.at[3])
    put_own.start()
    for h in range(2):
        w_plane(h, 2)
    a_near()
    a_far()
    lax.fori_loop(0, 64, pick_a, 0)
    over_tok(swap_a, "start")
    at[:, my_cols(t, 256)] = send_a[my_cols(t, 32), :]
    for h in range(2):
        w_along(h, 0)
    lax.fori_loop(8, 32, own_step, 0)
    t_forward()

    over_tok(swap_a, "recv")

    def rank_step(k, total):
        cols = my_cols(k, 1024)
        return total + mm(xv[:, cols], at[:, cols], NT)

    rank_in = lax.fori_loop(0, 8, rank_step, jnp.zeros((256, 32), F32))
    ri_s[...] = jnp.where(diagonal, rank_in, 0.0).astype(BF)
    for j in range(4):
        us[:, j * 256 : (j + 1) * 256] = (SCALE * mm(ri_s[...], go[j], TN)).astype(BF)
    over_tok(back_u, "start")
    ur[my_cols(t, 32), :] = us[:, my_cols(t // 4, 128)]

    for h in range(2):
        w_along(h, 1)
    for j in range(4):
        lo[:, j * 256 : (j + 1) * 256] = (
            SCALE * mm(ri_s[...], bt[:, j * 256 : (j + 1) * 256])
        ).astype(BF)

    over_tok(back_u, "recv")
    packed = jnp.zeros((256, 128), F32)
    for q in range(4):
        e = pick(((el >> 5) == (t & 3)) & ((ej >> 5) == q) & ((el & 31) == (ej & 31)))
        packed = packed + mm(ur[q * 256 : (q + 1) * 256, :], e)
    tu[f] = packed.astype(BF)
    u_start()

    def tile(row0):
        cols = pl.ds(pl.multiple_of(row0, 256), 256)
        xk = xv[:, cols]
        total = tga[:, cols] + mm(rg_s[...], at[:, cols])
        for fi in foreign:
            wk = wall[fi, cols, :]
            va[fi] += mm(xk, wk)
            total = total + mm(go[fi], wk, NT)
        tg_v[:, cols] = total.astype(BF)
        pltpu.make_async_copy(tg_v.at[:, cols], tgrad.at[:, cols], loc.at[2]).start()

    def tiles(d):
        def step(i, carry):
            h = i // 4
            pos = jnp.where(h == 0, lax.rem(x + d, 4), lax.rem(z + d, 4))
            tile(h * 4096 + pos * 1024 + (i % 4) * 256)
            return carry

        lax.fori_loop(0, 8, step, 0)

    def await_sibling(d):
        for h in range(2):
            for fi in range(3):
                for s in range(2):
                    wc[h, d, fi, s].wait_recv()

    for h in range(2):
        w_along(h, 2)
    await_sibling(0)
    tiles(0)
    u_forward()
    for fi in range(3):
        for h in range(2):
            for s in range(2):
                wx[h, 2, fi, s].wait_recv()
                to_sibling(foreign[fi], here(h, 2) + s * 256, (h, 2, fi, s))
    await_sibling(1)
    tiles(3)
    await_sibling(3)
    tiles(1)
    await_sibling(2)
    tiles(2)
    used = used_rows()
    for j in range(4):
        cols = slice(j * 256, (j + 1) * 256)
        values[:, cols] = jnp.where(used, va[j] + lo[:, cols].astype(F32), 0.0).astype(BF)
    t_near()
    t_far()
    puts = [put_own]
    for i, fi in enumerate(foreign):
        puts.append(pltpu.make_async_copy(te.at[fi], te_out.at[fi], loc.at[4 + i]))
        puts[-1].start()
    u_near()
    u_far()
    puts.append(pltpu.make_async_copy(tu, tu_out, loc.at[7]))
    puts[-1].start()

    pltpu.make_async_copy(tg_v, tgrad, loc.at[2]).wait()
    for copy in (swap_a, swap_b, back_t, back_u):
        over_tok(copy, "sent")
    for cp in pending:
        cp.wait_send()
    for cp in puts:
        cp.wait()


def sums(v_in, t_in, te, tu, tenant, fill, v_out, t_out, gdown, gup, v_s, t_s, acc, accu, cnt, sem):
    moves = [(v_in, v_s, v_out)]
    for i in range(8):
        rows = pl.ds(i * 32, 32)
        moves.append((t_in.at[rows, :], t_s.at[rows, :], t_out.at[rows, :]))
    loads = [pltpu.make_async_copy(a, b, sem.at[0, i]) for i, (a, b, _) in enumerate(moves)]
    stores = [pltpu.make_async_copy(b, c, sem.at[1, i]) for i, (_, b, c) in enumerate(moves)]
    for cp in loads:
        cp.start()
    f = lax.axis_index("fsdp")
    acc[...] = jnp.zeros_like(acc)
    accu[...] = jnp.zeros_like(accu)

    def clear(i, carry):
        cnt[i] = 0
        return carry

    lax.fori_loop(0, 65, clear, 0)
    lane32 = iota((16, 128), 1) >> 5

    def group(fi):
        def add(b, carry):
            g = tenant[fi * 64 + b] - f * 64
            slot = jnp.where((g >= 0) & (g < 64), g, 64)
            cnt[slot] = cnt[slot] + fill[fi * 64 + b]
            acc[slot] += te[fi, b].astype(F32)
            accu[slot] += jnp.where(lane32 == b // 16, tu[fi, b % 16].astype(F32), 0.0)
            return carry

        lax.fori_loop(0, 64, add, 0)

    group(0)
    for cp, out in zip(loads, stores):
        cp.wait()
        out.start()
    for fi in range(1, 4):
        group(fi)

    def mean(i, carry):
        n = jnp.maximum(cnt[i].astype(F32), 1.0)
        acc[i] = acc[i] / n
        accu[i] = accu[i] / n
        return carry

    lax.fori_loop(0, 64, mean, 0)
    for k in range(8):
        cols = slice(k * 128, (k + 1) * 128)
        gdown[:, cols] = acc[k * 8 : (k + 1) * 8].reshape(128, 256).T
        ut = accu[k * 8 : (k + 1) * 8].reshape(128, 128).T
        gup[:, cols] = ut[0:32] + ut[32:64] + ut[64:96] + ut[96:128]
    for cp in stores:
        cp.wait()


def local(tokens, weight, down, up, cotangent, tenant, fill):
    where = jnp.stack([tenant // 4, tenant % 4])
    any_ = pl.BlockSpec(memory_space=pl.ANY)
    vmem = pl.BlockSpec(memory_space=pltpu.VMEM)
    smem = pl.BlockSpec(memory_space=pltpu.SMEM)
    dma = pltpu.SemaphoreType.DMA
    V = pltpu.VMEM
    v_shape = jax.ShapeDtypeStruct((256, 1024), BF)
    t_shape = jax.ShapeDtypeStruct((256, 8192), BF)
    v, tg, te, tu = pl.pallas_call(
        kernel,
        out_shape=(
            v_shape,
            t_shape,
            jax.ShapeDtypeStruct((4, 1024, 256), BF),
            jax.ShapeDtypeStruct((4, 256, 128), BF),
        ),
        in_specs=[any_, any_, vmem, vmem, vmem, smem, smem, smem],
        out_specs=(vmem, any_, any_, any_),
        scratch_shapes=[
            V((256, 8192), BF),
            V((4, 8192, 256), BF),
            V((4, 256, 256), BF),
            V((4, 256, 256), F32),
            V((256, 8192), F32),
            V((256, 8192), BF),
            V((256, 16, 256), BF),
            V((64, 16, 128), BF),
            V((1024, 256), BF),
            V((1024, 128), BF),
            V((1024, 128), BF),
            V((32, 8192), BF),
            V((32, 32, 128), BF),
            V((32, 1024), BF),
            V((32, 8192), BF),
            V((32, 1024), BF),
            V((1024, 128), BF),
            V((4, 1024, 256), BF),
            V((4, 256, 128), BF),
            V((256, 1024), BF),
            V((256, 32), BF),
            V((256, 32), BF),
            dma((8,)),
            dma((2, 24)),
            dma((2, 12)),
            dma((2, 24)),
            dma((2, 36)),
            dma((2, 48)),
            dma((2, 32)),
            dma((2, 32)),
            dma((2, 32)),
            dma((2, 32)),
        ],
        compiler_params=pltpu.CompilerParams(
            has_side_effects=True, collective_id=1, vmem_limit_bytes=60 * 1024 * 1024
        ),
        cost_estimate=pl.CostEstimate(
            flops=9_000_000_000, bytes_accessed=30_000_000, transcendentals=0
        ),
    )(tokens, weight, down, up, cotangent, tenant, fill, where)
    return pl.pallas_call(
        sums,
        out_shape=(
            v_shape,
            t_shape,
            jax.ShapeDtypeStruct((256, 1024), F32),
            jax.ShapeDtypeStruct((32, 1024), F32),
        ),
        in_specs=[any_, any_, vmem, vmem, smem, smem],
        out_specs=(any_, any_, vmem, vmem),
        scratch_shapes=[
            V((256, 1024), BF),
            V((256, 8192), BF),
            V((65, 16, 256), F32),
            V((65, 16, 128), F32),
            pltpu.SMEM((65,), jnp.int32),
            dma((2, 9)),
        ],
        compiler_params=pltpu.CompilerParams(vmem_limit_bytes=32 * 1024 * 1024),
    )(v, tg, te.reshape(4, 64, 16, 256), tu.reshape(4, 16, 16, 128), tenant, fill)


def solution(mesh):
    placed = (
        P(("fsdp", "tok"), None),
        P(None, "fsdp"),
        P("tok", "fsdp"),
        P("tok", "fsdp"),
        P(("fsdp", "tok"), None),
        P(),
        P(),
    )
    return jax.shard_map(
        local,
        mesh=mesh,
        in_specs=placed,
        out_specs=(
            P(("fsdp", "tok"), None),
            P(("fsdp", "tok"), None),
            P("tok", "fsdp"),
            P("tok", "fsdp"),
        ),
        check_vma=False,
    )
```

```python
import jax
import jax.numpy as jnp
from jax import lax
from jax.experimental import pallas as pl
from jax.experimental.pallas import tpu as pltpu
from jax.sharding import PartitionSpec as P

RANK = 16
BLOCK = 128
SCALE = 2.0
BF = jnp.bfloat16
F32 = jnp.float32
NT = (((1,), (1,)), ((), ()))
TN = (((0,), (0,)), ((), ()))


def mm(a, b, dims=(((1,), (0,)), ((), ()))):
    return lax.dot_general(a, b, dims, preferred_element_type=F32)


def iota(shape, dim):
    return lax.broadcasted_iota(jnp.int32, shape, dim)


def pick(cond):
    return jnp.where(cond, 1.0, 0.0).astype(BF)


def kernel(
    x_hbm,
    w_hbm,
    down,
    upmap,
    cot,
    tenant,
    fill,
    values,
    tgrad,
    te_out,
    tu_out,
    xv,
    wall,
    go,
    va,
    tga,
    tg_v,
    ab_a,
    ab_b,
    send_a,
    vb,
    send_b,
    at,
    recv_b,
    bt,
    gs,
    us,
    ur,
    te,
    tu,
    lo,
    ri_s,
    rg_s,
    quarters,
    loc,
    y_sem,
    wy_sem,
    wx_sem,
    wc_sem,
    pa_sem,
    pb_sem,
    gt_sem,
    gu_sem,
):
    f = lax.axis_index("fsdp")
    t = lax.axis_index("tok")
    x = t // 8
    z = (t // 2) % 4
    c = t % 2

    def up(i, d):
        return lax.rem(i + d, 4)

    def dev_y(d):
        return (up(f, d), t)

    def dev_x(d):
        return (f, up(x, d) * 8 + z * 2 + c)

    def dev_z(d):
        return (f, x * 8 + up(z, d) * 2 + c)

    sibling = (f, x * 8 + z * 2 + (1 - c))

    def remote(src, dst, sem, i, dev):
        return pltpu.make_async_remote_copy(
            src_ref=src,
            dst_ref=dst,
            send_sem=sem.at[0, i],
            recv_sem=sem.at[1, i],
            device_id=dev,
            device_id_type=pl.DeviceIdType.MESH,
        )

    def my_cols(i, n):
        return pl.ds(pl.multiple_of(i * n, n), n)

    barrier = pltpu.get_barrier_semaphore()
    for d in (1, 3):
        pl.semaphore_signal(
            barrier, inc=1, device_id=dev_y(d), device_id_type=pl.DeviceIdType.MESH
        )

    def greet(d, carry):
        pl.semaphore_signal(
            barrier,
            inc=1,
            device_id=(f, lax.rem(t + d, 32)),
            device_id_type=pl.DeviceIdType.MESH,
        )
        return carry

    lax.fori_loop(1, 32, greet, 0)

    get_x = pltpu.make_async_copy(x_hbm, xv, loc.at[0])
    get_w = pltpu.make_async_copy(w_hbm, wall.at[f], loc.at[1])
    get_x.start()
    get_w.start()

    def quarter_step(i, carry):
        for k in range(4):
            quarters[4 * i + k] = i
        return carry

    lax.fori_loop(0, 64, quarter_step, 0)

    side = jnp.zeros((16, 16, 128), F32)
    for g in range(4):
        place = pick(iota((32, 128), 1) == iota((32, 128), 0) + 32 * g)
        moved = mm(upmap[...], place, TN).reshape(16, 64, 128)
        side = side + moved[:, g * 16 : (g + 1) * 16, :]
    ab_b[pl.ds(f * 16, 16)] = side.astype(BF)
    ab_a[pl.ds(f * 64, 64)] = down[...].astype(F32).T.astype(BF).reshape(64, 16, 256)

    pl.semaphore_wait(barrier, 33)

    pending = []

    def ring_y(part_of, sem, n0):
        first = {}
        last = []

        def start():
            for i, (d, s) in enumerate(((1, 0), (3, 1), (1, 1), (3, 0))):
                cp = remote(part_of(f, s), part_of(f, s), sem, n0 + i, dev_y(d))
                cp.start()
                first[d, s] = cp
                pending.append(cp)

        def forward():
            for i, (d, s) in enumerate(((1, 0), (3, 1))):
                first[d, s].wait_recv()
                src = up(f, 4 - d)
                cp = remote(
                    part_of(src, s), part_of(src, s), sem, n0 + 4 + i, dev_y(d)
                )
                cp.start()
                last.append(cp)
                pending.append(cp)

        def near():
            first[1, 1].wait_recv()
            first[3, 0].wait_recv()

        def far():
            for cp in last:
                cp.wait_recv()

        return start, forward, near, far

    b_start, b_forward, b_near, b_far = ring_y(
        lambda i, s: ab_b.at[pl.ds(i * 16 + s * 8, 8)], y_sem, 0
    )
    a_start, a_forward, a_near, a_far = ring_y(
        lambda i, s: ab_a.at[pl.ds(i * 64 + s * 32, 32)], y_sem, 6
    )
    t_start, t_forward, t_near, t_far = ring_y(
        lambda i, s: te.at[i, pl.ds(s * 512, 512)], y_sem, 12
    )
    u_start, u_forward, u_near, u_far = ring_y(
        lambda i, s: tu.at[i, pl.ds(s * 128, 128)], y_sem, 18
    )
    b_start()

    base = (x * 1024 + c * 512, 4096 + z * 1024 + c * 512)
    plane = (dev_x, dev_z)

    def wslice(fi, row0):
        return wall.at[fi, pl.ds(pl.multiple_of(row0, 256), 256), :]

    wy = {}
    n_y = 0
    for h in range(2):
        for d, s in ((1, 0), (3, 1), (1, 1), (3, 0)):
            r0 = base[h] + s * 256
            cp = remote(
                w_hbm.at[pl.ds(pl.multiple_of(r0, 256), 256), :],
                wslice(f, r0),
                wy_sem,
                n_y,
                dev_y(d),
            )
            cp.start()
            wy[h, d, s] = cp
            pending.append(cp)
            n_y += 1

    b0 = (f * 32 + t) * 2

    def used_rows():
        rows = iota((256, 1), 0)
        return rows < jnp.where(rows < BLOCK, fill[b0], fill[b0 + 1] + BLOCK)

    used = used_rows()
    for j in range(4):
        go[j] = jnp.where(used, cot[:, j * 256 : (j + 1) * 256].astype(F32), 0.0).astype(BF)

    b_forward()
    va[...] = jnp.zeros_like(va)
    b_near()

    wx = {}
    wc = {}
    fw = {}
    counters = {"x": 0, "c": 0}
    foreign = (up(f, 3), up(f, 1), up(f, 2))

    def same_place(fi, r0, sem, kind, dev):
        cp = remote(wslice(fi, r0), wslice(fi, r0), sem, counters[kind], dev)
        counters[kind] += 1
        cp.start()
        pending.append(cp)
        return cp

    def to_sibling(fi, r0, key):
        wc[key] = same_place(fi, r0, wc_sem, "c", sibling)

    def to_plane(fi, r0, d, key, h):
        wx[key] = same_place(fi, r0, wx_sem, "x", plane[h](d))

    def w_near(h):
        nonlocal n_y
        for d, s in ((1, 0), (3, 1)):
            wy[h, d, s].wait_recv()
            src = up(f, 4 - d)
            r0 = base[h] + s * 256
            cp = remote(wslice(src, r0), wslice(src, r0), wy_sem, n_y, dev_y(d))
            n_y += 1
            cp.start()
            fw[h, s] = cp
            pending.append(cp)
        for d, s in ((1, 0), (3, 1), (1, 1), (3, 0)):
            if (d, s) in ((1, 1), (3, 0)):
                wy[h, d, s].wait_recv()
            fi = 0 if d == 1 else 1
            r0 = base[h] + s * 256
            for dd in (1, 3) if s == 0 else (3, 1):
                to_plane(foreign[fi], r0, dd, (h, dd, fi, s), h)
            to_sibling(foreign[fi], r0, (h, 0, fi, s))

    def w_far(h):
        for s in range(2):
            fw[h, s].wait_recv()
            r0 = base[h] + s * 256
            for dd in (1, 3) if s == 0 else (3, 1):
                to_plane(foreign[2], r0, dd, (h, dd, 2, s), h)
            to_sibling(foreign[2], r0, (h, 0, 2, s))

    def here(h, d):
        if h == 0:
            return up(x, d) * 1024 + c * 512
        return 4096 + up(z, d) * 1024 + c * 512

    def w_along(h, fi):
        for d, s in ((1, 0), (3, 1)):
            wx[h, d, fi, s].wait_recv()
            r0 = here(h, 4 - d) + s * 256
            to_plane(foreign[fi], r0, d, (h, 2, fi, s), h)
            to_sibling(foreign[fi], r0, (h, d, fi, s))
        for d, s in ((1, 1), (3, 0)):
            wx[h, d, fi, s].wait_recv()
            r0 = here(h, 4 - d) + s * 256
            to_sibling(foreign[fi], r0, (h, d, fi, s))

    def w_end(h, fi):
        for s in range(2):
            wx[h, 2, fi, s].wait_recv()
            to_sibling(foreign[fi], here(h, 2) + s * 256, (h, 2, fi, s))

    b_far()

    lane32 = iota((16, 128), 1) >> 5
    el = iota((128, 128), 0)
    ej = iota((128, 128), 1)

    def pick_b(b, carry):
        quarter = quarters[tenant[f * 64 + b]]
        v = ab_b[quarter]
        vb[my_cols(b, 16), :] = jnp.where(
            lane32 == tenant[f * 64 + b] - 4 * quarter, v.astype(F32), 0.0
        ).astype(BF)
        return carry

    def pick_a(b, carry):
        send_a[my_cols(b, 16), :] = ab_a[tenant[f * 64 + b]]
        return carry

    def swap_a(d):
        to = lax.rem(t + d, 32)
        return remote(
            send_a.at[my_cols(to, 32), :], at.at[:, my_cols(t, 256)], pa_sem, d, (f, to)
        )

    def swap_b(d):
        to = lax.rem(t + d, 32)
        return remote(send_b.at[my_cols(to, 32), :], recv_b.at[t], pb_sem, d, (f, to))

    def back_t(d):
        to = lax.rem(t + d, 32)
        return remote(
            gs.at[:, my_cols(to, 256)], te.at[f, my_cols(t, 32), :], gt_sem, d, (f, to)
        )

    def back_u(d):
        to = lax.rem(t + d, 32)
        return remote(
            us.at[:, my_cols(to // 4, 128)], ur.at[my_cols(t, 32), :], gu_sem, d, (f, to)
        )

    def over_tok(copy, act):
        def step(d, carry):
            cp = copy(d)
            if act == "start":
                cp.start()
            elif act == "recv":
                cp.wait_recv()
            else:
                cp.wait_send()
            return carry

        lax.fori_loop(1, 32, step, 0)

    lax.fori_loop(0, 64, pick_b, 0)
    spread = pick(((el & 31) == (ej & 31)) & ((ej >> 5) == (t & 3)))
    send_b[...] = mm(vb[...], spread).astype(BF)
    over_tok(swap_b, "start")
    recv_b[t] = send_b[my_cols(t, 32), :]

    get_x.wait()
    w_near(0)

    over_tok(swap_b, "recv")
    for q in range(8):
        total = recv_b[4 * q]
        for i in range(1, 4):
            total = total + recv_b[4 * q + i]
        bt[:, q * 128 : (q + 1) * 128] = total
    diagonal = (iota((256, 32), 0) >> 7) == (iota((256, 32), 1) >> 4)
    rank_grad = jnp.zeros((256, 32), F32)
    for j in range(4):
        rank_grad = rank_grad + mm(go[j], bt[:, j * 256 : (j + 1) * 256], NT)
    rg_s[...] = jnp.where(diagonal, SCALE * rank_grad, 0.0).astype(BF)

    def terms_step(k, carry):
        cols = my_cols(k, 1024)
        gs[:, cols] = mm(rg_s[...], xv[:, cols], TN).astype(BF)
        return carry

    lax.fori_loop(0, 8, terms_step, 0)
    over_tok(back_t, "start")
    te[f, my_cols(t, 32), :] = gs[:, my_cols(t, 256)]

    w_near(1)
    a_start()
    get_w.wait()

    def own_step(k, carry):
        cols = my_cols(k, 256)
        wk = wall[f, cols, :]
        va[f] += mm(xv[:, cols], wk)
        tga[:, cols] = mm(go[f], wk, NT)
        return carry

    lax.fori_loop(0, 8, own_step, 0)
    for h in range(2):
        w_far(h)
    over_tok(back_t, "recv")
    put_own = pltpu.make_async_copy(te.at[f], te_out.at[f], loc.at[3])
    put_own.start()
    w_along(0, 0)
    a_forward()
    w_along(1, 0)
    a_near()
    t_start()
    lax.fori_loop(8, 20, own_step, 0)
    a_far()
    lax.fori_loop(0, 64, pick_a, 0)
    over_tok(swap_a, "start")
    at[:, my_cols(t, 256)] = send_a[my_cols(t, 32), :]
    w_along(0, 1)
    w_along(1, 1)
    t_forward()
    lax.fori_loop(20, 32, own_step, 0)

    over_tok(swap_a, "recv")

    def rank_step(k, total):
        cols = my_cols(k, 1024)
        return total + mm(xv[:, cols], at[:, cols], NT)

    rank_in = lax.fori_loop(0, 8, rank_step, jnp.zeros((256, 32), F32))
    ri_s[...] = jnp.where(diagonal, rank_in, 0.0).astype(BF)
    for j in range(4):
        us[:, j * 256 : (j + 1) * 256] = (SCALE * mm(ri_s[...], go[j], TN)).astype(BF)
    over_tok(back_u, "start")
    w_end(0, 0)
    w_end(1, 0)
    ur[my_cols(t, 32), :] = us[:, my_cols(t // 4, 128)]

    for j in range(4):
        lo[:, j * 256 : (j + 1) * 256] = (
            SCALE * mm(ri_s[...], bt[:, j * 256 : (j + 1) * 256])
        ).astype(BF)
    def tile(row0):
        cols = pl.ds(pl.multiple_of(row0, 256), 256)
        xk = xv[:, cols]
        total = tga[:, cols] + mm(rg_s[...], at[:, cols])
        for fi in foreign:
            wk = wall[fi, cols, :]
            va[fi] += mm(xk, wk)
            total = total + mm(go[fi], wk, NT)
        tg_v[:, cols] = total.astype(BF)
        pltpu.make_async_copy(tg_v.at[:, cols], tgrad.at[:, cols], loc.at[2]).start()

    def tiles(d):
        def step(i, carry):
            h = i // 4
            pos = jnp.where(h == 0, lax.rem(x + d, 4), lax.rem(z + d, 4))
            tile(h * 4096 + pos * 1024 + (i % 4) * 256)
            return carry

        lax.fori_loop(0, 8, step, 0)

    def await_sibling(d):
        for h in range(2):
            for fi in range(3):
                for s in range(2):
                    wc[h, d, fi, s].wait_recv()

    over_tok(back_u, "recv")
    packed = jnp.zeros((256, 128), F32)
    for q in range(4):
        e = pick(((el >> 5) == (t & 3)) & ((ej >> 5) == q) & ((el & 31) == (ej & 31)))
        packed = packed + mm(ur[q * 256 : (q + 1) * 256, :], e)
    tu[f] = packed.astype(BF)
    u_start()
    w_along(0, 2)
    w_along(1, 2)
    await_sibling(0)
    tiles(0)
    w_end(0, 1)
    w_end(1, 1)
    u_forward()
    await_sibling(1)
    tiles(3)
    t_near()
    puts = [put_own]
    for i, fi in enumerate(foreign[:2]):
        puts.append(pltpu.make_async_copy(te.at[fi], te_out.at[fi], loc.at[4 + i]))
        puts[-1].start()
    w_end(0, 2)
    w_end(1, 2)
    await_sibling(3)
    tiles(1)
    await_sibling(2)
    tiles(2)
    used = used_rows()
    for j in range(4):
        cols = slice(j * 256, (j + 1) * 256)
        values[:, cols] = jnp.where(used, va[j] + lo[:, cols].astype(F32), 0.0).astype(BF)
    t_far()
    puts.append(pltpu.make_async_copy(te.at[foreign[2]], te_out.at[foreign[2]], loc.at[6]))
    puts[-1].start()
    u_near()
    u_far()
    puts.append(pltpu.make_async_copy(tu, tu_out, loc.at[7]))
    puts[-1].start()

    pltpu.make_async_copy(tg_v, tgrad, loc.at[2]).wait()
    for copy in (swap_a, swap_b, back_t, back_u):
        over_tok(copy, "sent")
    for cp in pending:
        cp.wait_send()
    for cp in puts:
        cp.wait()


def sums(v_in, t_in, te_in, tu_in, tenant, fill, v_out, t_out, gdown, gup, *scratch):
    v_s, t_s, te, tu, acc, accu, cnt, mine, sem = scratch
    first = [
        pltpu.make_async_copy(te_in, te, sem.at[0, 9]),
        pltpu.make_async_copy(tu_in, tu, sem.at[0, 10]),
    ]
    moves = [(v_in, v_s, v_out)]
    for i in range(8):
        rows = pl.ds(i * 32, 32)
        moves.append((t_in.at[rows, :], t_s.at[rows, :], t_out.at[rows, :]))
    loads = [pltpu.make_async_copy(a, b, sem.at[0, i]) for i, (a, b, _) in enumerate(moves)]
    stores = [pltpu.make_async_copy(b, c, sem.at[1, i]) for i, (_, b, c) in enumerate(moves)]
    for cp in first + loads:
        cp.start()
    f = lax.axis_index("fsdp")
    acc[...] = jnp.zeros_like(acc)
    accu[...] = jnp.zeros_like(accu)

    def clear(i, carry):
        cnt[i] = 0
        return carry

    lax.fori_loop(0, 65, clear, 0)

    def note(b, n):
        g = tenant[b] - f * 64
        own = (g >= 0) & (g < 64)
        slot = jnp.where(own, g, 64)
        cnt[slot] = cnt[slot] + fill[b]
        mine[n] = b
        return n + jnp.where(own, 1, 0)

    count = lax.fori_loop(0, 256, note, 0)
    lane32 = iota((16, 128), 1) >> 5
    for cp in first:
        cp.wait()
    for cp, out in zip(loads, stores):
        cp.wait()
        out.start()

    def add(i, carry):
        b = mine[i]
        slot = tenant[b] - f * 64
        fi = b // 64
        k = b % 64
        acc[slot] += te[fi, k].astype(F32)
        accu[slot] += jnp.where(lane32 == k // 16, tu[fi, k % 16].astype(F32), 0.0)
        return carry

    lax.fori_loop(0, count, add, 0)

    def mean(i, carry):
        n = jnp.maximum(cnt[i].astype(F32), 1.0)
        acc[i] = acc[i] / n
        accu[i] = accu[i] / n
        return carry

    lax.fori_loop(0, 64, mean, 0, unroll=4)
    for k in range(8):
        cols = slice(k * 128, (k + 1) * 128)
        gdown[:, cols] = acc[k * 8 : (k + 1) * 8].reshape(128, 256).T
        ut = accu[k * 8 : (k + 1) * 8].reshape(128, 128).T
        gup[:, cols] = ut[0:32] + ut[32:64] + ut[64:96] + ut[96:128]
    for cp in stores:
        cp.wait()


def local(tokens, weight, down, up, cotangent, tenant, fill):
    any_ = pl.BlockSpec(memory_space=pl.ANY)
    vmem = pl.BlockSpec(memory_space=pltpu.VMEM)
    smem = pl.BlockSpec(memory_space=pltpu.SMEM)
    dma = pltpu.SemaphoreType.DMA
    V = pltpu.VMEM
    v_shape = jax.ShapeDtypeStruct((256, 1024), BF)
    t_shape = jax.ShapeDtypeStruct((256, 8192), BF)
    v, tg, te, tu = pl.pallas_call(
        kernel,
        out_shape=(
            v_shape,
            t_shape,
            jax.ShapeDtypeStruct((4, 1024, 256), BF),
            jax.ShapeDtypeStruct((4, 256, 128), BF),
        ),
        in_specs=[any_, any_, vmem, vmem, vmem, smem, smem],
        out_specs=(vmem, any_, any_, any_),
        scratch_shapes=[
            V((256, 8192), BF),
            V((4, 8192, 256), BF),
            V((4, 256, 256), BF),
            V((4, 256, 256), F32),
            V((256, 8192), F32),
            V((256, 8192), BF),
            V((256, 16, 256), BF),
            V((64, 16, 128), BF),
            V((1024, 256), BF),
            V((1024, 128), BF),
            V((1024, 128), BF),
            V((32, 8192), BF),
            V((32, 32, 128), BF),
            V((32, 1024), BF),
            V((32, 8192), BF),
            V((32, 1024), BF),
            V((1024, 128), BF),
            V((4, 1024, 256), BF),
            V((4, 256, 128), BF),
            V((256, 1024), BF),
            V((256, 32), BF),
            V((256, 32), BF),
            pltpu.SMEM((256,), jnp.int32),
            dma((8,)),
            dma((2, 24)),
            dma((2, 12)),
            dma((2, 36)),
            dma((2, 48)),
            dma((2, 32)),
            dma((2, 32)),
            dma((2, 32)),
            dma((2, 32)),
        ],
        compiler_params=pltpu.CompilerParams(
            has_side_effects=True, collective_id=1, vmem_limit_bytes=60 * 1024 * 1024
        ),
        cost_estimate=pl.CostEstimate(
            flops=9_000_000_000, bytes_accessed=30_000_000, transcendentals=0
        ),
    )(tokens, weight, down, up, cotangent, tenant, fill)
    return pl.pallas_call(
        sums,
        out_shape=(
            v_shape,
            t_shape,
            jax.ShapeDtypeStruct((256, 1024), F32),
            jax.ShapeDtypeStruct((32, 1024), F32),
        ),
        in_specs=[any_, any_, any_, any_, smem, smem],
        out_specs=(any_, any_, vmem, vmem),
        scratch_shapes=[
            V((256, 1024), BF),
            V((256, 8192), BF),
            V((4, 64, 16, 256), BF),
            V((4, 16, 16, 128), BF),
            V((65, 16, 256), F32),
            V((65, 16, 128), F32),
            pltpu.SMEM((65,), jnp.int32),
            pltpu.SMEM((256,), jnp.int32),
            dma((2, 11)),
        ],
        compiler_params=pltpu.CompilerParams(vmem_limit_bytes=60 * 1024 * 1024),
    )(v, tg, te.reshape(4, 64, 16, 256), tu.reshape(4, 16, 16, 128), tenant, fill)


def solution(mesh):
    placed = (
        P(("fsdp", "tok"), None),
        P(None, "fsdp"),
        P("tok", "fsdp"),
        P("tok", "fsdp"),
        P(("fsdp", "tok"), None),
        P(),
        P(),
    )
    return jax.shard_map(
        local,
        mesh=mesh,
        in_specs=placed,
        out_specs=(
            P(("fsdp", "tok"), None),
            P(("fsdp", "tok"), None),
            P("tok", "fsdp"),
            P("tok", "fsdp"),
        ),
        check_vma=False,
    )
```

```python
import jax
import jax.numpy as jnp
from jax import lax
from jax.experimental import pallas as pl
from jax.experimental.pallas import tpu as pltpu
from jax.sharding import PartitionSpec as P

RANK = 16
BLOCK = 128
SCALE = 2.0
BF = jnp.bfloat16
F32 = jnp.float32
NT = (((1,), (1,)), ((), ()))
TN = (((0,), (0,)), ((), ()))


def mm(a, b, dims=(((1,), (0,)), ((), ()))):
    return lax.dot_general(a, b, dims, preferred_element_type=F32)


def iota(shape, dim):
    return lax.broadcasted_iota(jnp.int32, shape, dim)


def pick(cond):
    return jnp.where(cond, 1.0, 0.0).astype(BF)


def kernel(
    x_hbm,
    w_hbm,
    down,
    upmap,
    cot,
    tenant,
    fill,
    values,
    tgrad,
    te_out,
    tu_out,
    xv,
    wall,
    go,
    va,
    tga,
    tg_v,
    ab_a,
    ab_b,
    send_a,
    vb,
    send_b,
    at,
    recv_b,
    bt,
    gs,
    us,
    usj,
    ur,
    te,
    tu,
    lo,
    ri_s,
    rg_s,
    quarters,
    loc,
    y_sem,
    wy_sem,
    wx_sem,
    wc_sem,
    pa_sem,
    pb_sem,
    gt_sem,
    gu_sem,
):
    f = lax.axis_index("fsdp")
    t = lax.axis_index("tok")
    x = t // 8
    z = (t // 2) % 4
    c = t % 2

    def up(i, d):
        return lax.rem(i + d, 4)

    def dev_y(d):
        return (up(f, d), t)

    def dev_x(d):
        return (f, up(x, d) * 8 + z * 2 + c)

    def dev_z(d):
        return (f, x * 8 + up(z, d) * 2 + c)

    sibling = (f, x * 8 + z * 2 + (1 - c))

    def remote(src, dst, sem, i, dev):
        return pltpu.make_async_remote_copy(
            src_ref=src,
            dst_ref=dst,
            send_sem=sem.at[0, i],
            recv_sem=sem.at[1, i],
            device_id=dev,
            device_id_type=pl.DeviceIdType.MESH,
        )

    def my_cols(i, n):
        return pl.ds(pl.multiple_of(i * n, n), n)

    barrier = pltpu.get_barrier_semaphore()
    for d in (1, 3):
        pl.semaphore_signal(
            barrier, inc=1, device_id=dev_y(d), device_id_type=pl.DeviceIdType.MESH
        )

    def greet(d, carry):
        pl.semaphore_signal(
            barrier,
            inc=1,
            device_id=(f, lax.rem(t + d, 32)),
            device_id_type=pl.DeviceIdType.MESH,
        )
        return carry

    lax.fori_loop(1, 32, greet, 0)

    get_x = pltpu.make_async_copy(x_hbm, xv, loc.at[0])
    get_w = pltpu.make_async_copy(w_hbm, wall.at[f], loc.at[1])
    get_x.start()
    get_w.start()

    def quarter_step(i, carry):
        for k in range(4):
            quarters[4 * i + k] = i
        return carry

    lax.fori_loop(0, 64, quarter_step, 0)

    side = jnp.zeros((16, 16, 128), F32)
    for g in range(4):
        place = pick(iota((32, 128), 1) == iota((32, 128), 0) + 32 * g)
        moved = mm(upmap[...], place, TN).reshape(16, 64, 128)
        side = side + moved[:, g * 16 : (g + 1) * 16, :]
    ab_b[pl.ds(f * 16, 16)] = side.astype(BF)

    pl.semaphore_wait(barrier, 33)

    pending = []

    def ring_y(part_of, sem, n0):
        first = {}
        last = []

        def start():
            for i, (d, s) in enumerate(((1, 0), (3, 1), (1, 1), (3, 0))):
                cp = remote(part_of(f, s), part_of(f, s), sem, n0 + i, dev_y(d))
                cp.start()
                first[d, s] = cp
                pending.append(cp)

        def forward():
            for i, (d, s) in enumerate(((1, 0), (3, 1))):
                first[d, s].wait_recv()
                src = up(f, 4 - d)
                cp = remote(
                    part_of(src, s), part_of(src, s), sem, n0 + 4 + i, dev_y(d)
                )
                cp.start()
                last.append(cp)
                pending.append(cp)

        def near():
            first[1, 1].wait_recv()
            first[3, 0].wait_recv()

        def far():
            for cp in last:
                cp.wait_recv()

        return start, forward, near, far

    b_start, b_forward, b_near, b_far = ring_y(
        lambda i, s: ab_b.at[pl.ds(i * 16 + s * 8, 8)], y_sem, 0
    )
    a_start, a_forward, a_near, a_far = ring_y(
        lambda i, s: ab_a.at[pl.ds(i * 64 + s * 32, 32)], y_sem, 6
    )
    t_start, t_forward, t_near, t_far = ring_y(
        lambda i, s: te.at[i, pl.ds(s * 512, 512)], y_sem, 12
    )
    u_start, u_forward, u_near, u_far = ring_y(
        lambda i, s: tu.at[i, pl.ds(s * 128, 128)], y_sem, 18
    )
    b_start()

    base = (x * 1024 + c * 512, 4096 + z * 1024 + c * 512)
    plane = (dev_x, dev_z)

    def wslice(fi, row0):
        return wall.at[fi, pl.ds(pl.multiple_of(row0, 256), 256), :]

    wy = {}
    n_y = 0

    def wy_start(h):
        nonlocal n_y
        for d, s in ((1, 0), (3, 1), (1, 1), (3, 0)):
            r0 = base[h] + s * 256
            cp = remote(
                w_hbm.at[pl.ds(pl.multiple_of(r0, 256), 256), :],
                wslice(f, r0),
                wy_sem,
                n_y,
                dev_y(d),
            )
            cp.start()
            wy[h, d, s] = cp
            pending.append(cp)
            n_y += 1

    wy_start(0)
    ab_a[pl.ds(f * 64, 64)] = down[...].astype(F32).T.astype(BF).reshape(64, 16, 256)

    b0 = (f * 32 + t) * 2

    def used_rows():
        rows = iota((256, 1), 0)
        return rows < jnp.where(rows < BLOCK, fill[b0], fill[b0 + 1] + BLOCK)

    used = used_rows()
    for j in range(4):
        go[j] = jnp.where(used, cot[:, j * 256 : (j + 1) * 256].astype(F32), 0.0).astype(BF)

    b_forward()
    va[...] = jnp.zeros_like(va)
    b_near()

    wx = {}
    wc = {}
    fw = {}
    counters = {"x": 0, "c": 0}
    foreign = (up(f, 3), up(f, 1), up(f, 2))

    def same_place(fi, r0, sem, kind, dev):
        cp = remote(wslice(fi, r0), wslice(fi, r0), sem, counters[kind], dev)
        counters[kind] += 1
        cp.start()
        pending.append(cp)
        return cp

    def to_sibling(fi, r0, key):
        wc[key] = same_place(fi, r0, wc_sem, "c", sibling)

    def to_plane(fi, r0, d, key, h):
        wx[key] = same_place(fi, r0, wx_sem, "x", plane[h](d))

    def w_near(h):
        nonlocal n_y
        for d, s in ((1, 0), (3, 1)):
            wy[h, d, s].wait_recv()
            src = up(f, 4 - d)
            r0 = base[h] + s * 256
            cp = remote(wslice(src, r0), wslice(src, r0), wy_sem, n_y, dev_y(d))
            n_y += 1
            cp.start()
            fw[h, s] = cp
            pending.append(cp)
        for d, s in ((1, 0), (3, 1), (1, 1), (3, 0)):
            if (d, s) in ((1, 1), (3, 0)):
                wy[h, d, s].wait_recv()
            fi = 0 if d == 1 else 1
            r0 = base[h] + s * 256
            for dd in (1, 3) if s == 0 else (3, 1):
                to_plane(foreign[fi], r0, dd, (h, dd, fi, s), h)
            to_sibling(foreign[fi], r0, (h, 0, fi, s))

    def w_far(h):
        for s in range(2):
            fw[h, s].wait_recv()
            r0 = base[h] + s * 256
            for dd in (1, 3) if s == 0 else (3, 1):
                to_plane(foreign[2], r0, dd, (h, dd, 2, s), h)
            to_sibling(foreign[2], r0, (h, 0, 2, s))

    def here(h, d):
        if h == 0:
            return up(x, d) * 1024 + c * 512
        return 4096 + up(z, d) * 1024 + c * 512

    def w_along(h, fi):
        for d, s in ((1, 0), (3, 1)):
            wx[h, d, fi, s].wait_recv()
            r0 = here(h, 4 - d) + s * 256
            to_plane(foreign[fi], r0, d, (h, 2, fi, s), h)
            to_sibling(foreign[fi], r0, (h, d, fi, s))
        for d, s in ((1, 1), (3, 0)):
            wx[h, d, fi, s].wait_recv()
            r0 = here(h, 4 - d) + s * 256
            to_sibling(foreign[fi], r0, (h, d, fi, s))

    def w_end(h, fi):
        for s in range(2):
            wx[h, 2, fi, s].wait_recv()
            to_sibling(foreign[fi], here(h, 2) + s * 256, (h, 2, fi, s))

    b_far()

    lane32 = iota((16, 128), 1) >> 5
    el = iota((128, 128), 0)
    ej = iota((128, 128), 1)

    def pick_b(i, carry):
        for j in range(2):
            g = tenant[f * 64 + 2 * i + j]
            quarter = quarters[g]
            v = ab_b[quarter]
            vb[j, my_cols(i, 16), :] = jnp.where(
                lane32 == g - 4 * quarter, v.astype(F32), 0.0
            ).astype(BF)
        return carry

    def lanes(i, j):
        return pick((el == i * 32 + (ej & 31)) & ((ej >> 5) == j))

    def pick_a(b, carry):
        send_a[my_cols(b, 16), :] = ab_a[tenant[f * 64 + b]]
        return carry

    def swap_a(d):
        to = lax.rem(t + d, 32)
        return remote(
            send_a.at[my_cols(to, 32), :], at.at[:, my_cols(t, 256)], pa_sem, d, (f, to)
        )

    def swap_b(d):
        to = lax.rem(t + d, 32)
        return remote(send_b.at[to], recv_b.at[t // 4, t % 4], pb_sem, d, (f, to))

    def back_t(d):
        to = lax.rem(t + d, 32)
        return remote(
            gs.at[:, my_cols(to, 256)], te.at[f, my_cols(t, 32), :], gt_sem, d, (f, to)
        )

    def back_u(d):
        to = lax.rem(t + d, 32)
        return remote(
            us.at[to // 4, to % 4], ur.at[t // 4, t % 4], gu_sem, d, (f, to)
        )

    def over_tok(copy, act):
        def step(d, carry):
            cp = copy(d)
            if act == "start":
                cp.start()
            elif act == "recv":
                cp.wait_recv()
            else:
                cp.wait_send()
            return carry

        lax.fori_loop(1, 32, step, 0)

    lax.fori_loop(0, 32, pick_b, 0)
    for j in range(2):
        spread = pick(((el & 31) == (ej & 31)) & ((ej >> 5) == j))
        moved = mm(vb[j], spread)
        side = moved if j == 0 else side + moved
    send_b[...] = side.astype(BF).reshape(32, 16, 128)
    over_tok(swap_b, "start")
    recv_b[t // 4, t % 4] = send_b[t]

    wy_start(1)
    get_x.wait()
    w_near(0)

    over_tok(swap_b, "recv")
    for j in range(2):
        total = jnp.zeros((128, 128), F32)
        for i in range(4):
            total = total + mm(recv_b[:, i].reshape(128, 128), lanes(j, i))
        for q in range(8):
            bt[j * 16 : (j + 1) * 16, q * 128 : (q + 1) * 128] = total[
                q * 16 : (q + 1) * 16, :
            ].astype(BF)
    diagonal = (iota((256, 32), 0) >> 7) == (iota((256, 32), 1) >> 4)
    rank_grad = jnp.zeros((256, 32), F32)
    for j in range(4):
        rank_grad = rank_grad + mm(go[j], bt[:, j * 256 : (j + 1) * 256], NT)
    rg_s[...] = jnp.where(diagonal, SCALE * rank_grad, 0.0).astype(BF)

    def terms_step(k, carry):
        cols = my_cols(k, 1024)
        gs[:, cols] = mm(rg_s[...], xv[:, cols], TN).astype(BF)
        return carry

    lax.fori_loop(0, 8, terms_step, 0)
    over_tok(back_t, "start")
    te[f, my_cols(t, 32), :] = gs[:, my_cols(t, 256)]

    w_near(1)
    a_start()
    get_w.wait()

    def own_step(k, carry):
        cols = my_cols(k, 256)
        wk = wall[f, cols, :]
        va[f] += mm(xv[:, cols], wk)
        tga[:, cols] = mm(go[f], wk, NT)
        return carry

    lax.fori_loop(0, 8, own_step, 0)
    for h in range(2):
        w_far(h)
    over_tok(back_t, "recv")
    put_own = pltpu.make_async_copy(te.at[f], te_out.at[f], loc.at[3])
    put_own.start()
    w_along(0, 0)
    a_forward()
    w_along(1, 0)
    a_near()
    t_start()
    lax.fori_loop(8, 20, own_step, 0)
    a_far()
    lax.fori_loop(0, 64, pick_a, 0)
    over_tok(swap_a, "start")
    at[:, my_cols(t, 256)] = send_a[my_cols(t, 32), :]
    w_along(0, 1)
    w_along(1, 1)
    t_forward()
    lax.fori_loop(20, 32, own_step, 0)

    over_tok(swap_a, "recv")

    def rank_step(k, total):
        cols = my_cols(k, 1024)
        return total + mm(xv[:, cols], at[:, cols], NT)

    rank_in = lax.fori_loop(0, 8, rank_step, jnp.zeros((256, 32), F32))
    ri_s[...] = jnp.where(diagonal, rank_in, 0.0).astype(BF)
    for k in range(4):
        part = (SCALE * mm(ri_s[...], go[k], TN)).astype(BF)
        for q in range(2):
            for j in range(2):
                usj[j, (2 * k + q) * 16 : (2 * k + q + 1) * 16, :] = part[
                    j * 16 : (j + 1) * 16, q * 128 : (q + 1) * 128
                ]
    for i in range(4):
        part = mm(usj[0], lanes(i, 0)) + mm(usj[1], lanes(i, 1))
        us[:, i] = part.astype(BF).reshape(8, 16, 128)
    over_tok(back_u, "start")
    w_end(0, 0)
    w_end(1, 0)
    ur[t // 4, t % 4] = us[t // 4, t % 4]

    for j in range(4):
        lo[:, j * 256 : (j + 1) * 256] = (
            SCALE * mm(ri_s[...], bt[:, j * 256 : (j + 1) * 256])
        ).astype(BF)
    def tile(row0):
        cols = pl.ds(pl.multiple_of(row0, 256), 256)
        xk = xv[:, cols]
        total = tga[:, cols] + mm(rg_s[...], at[:, cols])
        for fi in foreign:
            wk = wall[fi, cols, :]
            va[fi] += mm(xk, wk)
            total = total + mm(go[fi], wk, NT)
        tg_v[:, cols] = total.astype(BF)
        pltpu.make_async_copy(tg_v.at[:, cols], tgrad.at[:, cols], loc.at[2]).start()

    def tiles(d):
        def step(i, carry):
            h = i // 4
            pos = jnp.where(h == 0, lax.rem(x + d, 4), lax.rem(z + d, 4))
            tile(h * 4096 + pos * 1024 + (i % 4) * 256)
            return carry

        lax.fori_loop(0, 8, step, 0)

    def await_sibling(d):
        for h in range(2):
            for fi in range(3):
                for s in range(2):
                    wc[h, d, fi, s].wait_recv()

    over_tok(back_u, "recv")
    for j in range(2):
        packed = jnp.zeros((128, 128), F32)
        for q in range(4):
            packed = packed + mm(ur[2 * q : 2 * q + 2].reshape(128, 128), lanes(j, q))
        tu[f, j * 128 : (j + 1) * 128, :] = packed.astype(BF)
    u_start()
    w_along(0, 2)
    w_along(1, 2)
    await_sibling(0)
    tiles(0)
    w_end(0, 1)
    w_end(1, 1)
    u_forward()
    await_sibling(1)
    tiles(3)
    t_near()
    puts = [put_own]
    for i, fi in enumerate(foreign[:2]):
        puts.append(pltpu.make_async_copy(te.at[fi], te_out.at[fi], loc.at[4 + i]))
        puts[-1].start()
    w_end(0, 2)
    w_end(1, 2)
    await_sibling(3)
    tiles(1)
    await_sibling(2)
    tiles(2)
    used = used_rows()
    for j in range(4):
        cols = slice(j * 256, (j + 1) * 256)
        values[:, cols] = jnp.where(used, va[j] + lo[:, cols].astype(F32), 0.0).astype(BF)
    t_far()
    puts.append(pltpu.make_async_copy(te.at[foreign[2]], te_out.at[foreign[2]], loc.at[6]))
    puts[-1].start()
    u_near()
    u_far()
    puts.append(pltpu.make_async_copy(tu, tu_out, loc.at[7]))
    puts[-1].start()

    pltpu.make_async_copy(tg_v, tgrad, loc.at[2]).wait()
    for copy in (swap_a, swap_b, back_t, back_u):
        over_tok(copy, "sent")
    for cp in pending:
        cp.wait_send()
    for cp in puts:
        cp.wait()


def sums(v_in, t_in, te_in, tu_in, tenant, fill, v_out, t_out, gdown, gup, *scratch):
    v_s, t_s, te, tu, acc, accu, cnt, mine, sem = scratch
    first = [
        pltpu.make_async_copy(te_in, te, sem.at[0, 9]),
        pltpu.make_async_copy(tu_in, tu, sem.at[0, 10]),
    ]
    moves = [(v_in, v_s, v_out)]
    for i in range(8):
        rows = pl.ds(i * 32, 32)
        moves.append((t_in.at[rows, :], t_s.at[rows, :], t_out.at[rows, :]))
    loads = [pltpu.make_async_copy(a, b, sem.at[0, i]) for i, (a, b, _) in enumerate(moves)]
    stores = [pltpu.make_async_copy(b, c, sem.at[1, i]) for i, (_, b, c) in enumerate(moves)]
    for cp in first + loads:
        cp.start()
    f = lax.axis_index("fsdp")
    acc[...] = jnp.zeros_like(acc)
    accu[...] = jnp.zeros_like(accu)

    def clear(i, carry):
        cnt[i] = 0
        return carry

    lax.fori_loop(0, 65, clear, 0)

    def note(b, n):
        g = tenant[b] - f * 64
        own = (g >= 0) & (g < 64)
        slot = jnp.where(own, g, 64)
        cnt[slot] = cnt[slot] + fill[b]
        mine[n] = b
        return n + jnp.where(own, 1, 0)

    count = lax.fori_loop(0, 256, note, 0)
    lane32 = iota((16, 128), 1) >> 5
    for cp in first:
        cp.wait()
    for cp, out in zip(loads, stores):
        cp.wait()
        out.start()

    def add(i, carry):
        b = mine[i]
        slot = tenant[b] - f * 64
        fi = b // 64
        k = b % 64
        acc[slot] += te[fi, k].astype(F32)
        accu[slot] += jnp.where(lane32 == k // 16, tu[fi, (k % 2) * 8 + (k % 16) // 2].astype(F32), 0.0)
        return carry

    lax.fori_loop(0, count, add, 0)

    def mean(i, carry):
        n = jnp.maximum(cnt[i].astype(F32), 1.0)
        acc[i] = acc[i] / n
        accu[i] = accu[i] / n
        return carry

    lax.fori_loop(0, 64, mean, 0, unroll=4)
    for k in range(8):
        cols = slice(k * 128, (k + 1) * 128)
        gdown[:, cols] = acc[k * 8 : (k + 1) * 8].reshape(128, 256).T
        ut = accu[k * 8 : (k + 1) * 8].reshape(128, 128).T
        gup[:, cols] = ut[0:32] + ut[32:64] + ut[64:96] + ut[96:128]
    for cp in stores:
        cp.wait()


def local(tokens, weight, down, up, cotangent, tenant, fill):
    any_ = pl.BlockSpec(memory_space=pl.ANY)
    vmem = pl.BlockSpec(memory_space=pltpu.VMEM)
    smem = pl.BlockSpec(memory_space=pltpu.SMEM)
    dma = pltpu.SemaphoreType.DMA
    V = pltpu.VMEM
    v_shape = jax.ShapeDtypeStruct((256, 1024), BF)
    t_shape = jax.ShapeDtypeStruct((256, 8192), BF)
    v, tg, te, tu = pl.pallas_call(
        kernel,
        out_shape=(
            v_shape,
            t_shape,
            jax.ShapeDtypeStruct((4, 1024, 256), BF),
            jax.ShapeDtypeStruct((4, 256, 128), BF),
        ),
        in_specs=[any_, any_, vmem, vmem, vmem, smem, smem],
        out_specs=(vmem, any_, any_, any_),
        scratch_shapes=[
            V((256, 8192), BF),
            V((4, 8192, 256), BF),
            V((4, 256, 256), BF),
            V((4, 256, 256), F32),
            V((256, 8192), F32),
            V((256, 8192), BF),
            V((256, 16, 256), BF),
            V((64, 16, 128), BF),
            V((1024, 256), BF),
            V((2, 512, 128), BF),
            V((32, 16, 128), BF),
            V((32, 8192), BF),
            V((8, 4, 16, 128), BF),
            V((32, 1024), BF),
            V((32, 8192), BF),
            V((8, 4, 16, 128), BF),
            V((2, 128, 128), BF),
            V((8, 4, 16, 128), BF),
            V((4, 1024, 256), BF),
            V((4, 256, 128), BF),
            V((256, 1024), BF),
            V((256, 32), BF),
            V((256, 32), BF),
            pltpu.SMEM((256,), jnp.int32),
            dma((8,)),
            dma((2, 24)),
            dma((2, 12)),
            dma((2, 36)),
            dma((2, 48)),
            dma((2, 32)),
            dma((2, 32)),
            dma((2, 32)),
            dma((2, 32)),
        ],
        compiler_params=pltpu.CompilerParams(
            has_side_effects=True, collective_id=1, vmem_limit_bytes=60 * 1024 * 1024
        ),
        cost_estimate=pl.CostEstimate(
            flops=9_000_000_000, bytes_accessed=30_000_000, transcendentals=0
        ),
    )(tokens, weight, down, up, cotangent, tenant, fill)
    return pl.pallas_call(
        sums,
        out_shape=(
            v_shape,
            t_shape,
            jax.ShapeDtypeStruct((256, 1024), F32),
            jax.ShapeDtypeStruct((32, 1024), F32),
        ),
        in_specs=[any_, any_, any_, any_, smem, smem],
        out_specs=(any_, any_, vmem, vmem),
        scratch_shapes=[
            V((256, 1024), BF),
            V((256, 8192), BF),
            V((4, 64, 16, 256), BF),
            V((4, 16, 16, 128), BF),
            V((65, 16, 256), F32),
            V((65, 16, 128), F32),
            pltpu.SMEM((65,), jnp.int32),
            pltpu.SMEM((256,), jnp.int32),
            dma((2, 11)),
        ],
        compiler_params=pltpu.CompilerParams(vmem_limit_bytes=60 * 1024 * 1024),
    )(v, tg, te.reshape(4, 64, 16, 256), tu.reshape(4, 16, 16, 128), tenant, fill)


def solution(mesh):
    placed = (
        P(("fsdp", "tok"), None),
        P(None, "fsdp"),
        P("tok", "fsdp"),
        P("tok", "fsdp"),
        P(("fsdp", "tok"), None),
        P(),
        P(),
    )
    return jax.shard_map(
        local,
        mesh=mesh,
        in_specs=placed,
        out_specs=(
            P(("fsdp", "tok"), None),
            P(("fsdp", "tok"), None),
            P("tok", "fsdp"),
            P("tok", "fsdp"),
        ),
        check_vma=False,
    )
```

```python
import jax
import jax.numpy as jnp
from jax import lax
from jax.experimental import pallas as pl
from jax.experimental.pallas import tpu as pltpu
from jax.sharding import PartitionSpec as P

RANK = 16
BLOCK = 128
SCALE = 2.0
BF = jnp.bfloat16
F32 = jnp.float32
NT = (((1,), (1,)), ((), ()))
TN = (((0,), (0,)), ((), ()))


def mm(a, b, dims=(((1,), (0,)), ((), ()))):
    return lax.dot_general(a, b, dims, preferred_element_type=F32)


def iota(shape, dim):
    return lax.broadcasted_iota(jnp.int32, shape, dim)


def pick(cond):
    return jnp.where(cond, 1.0, 0.0).astype(BF)


def kernel(
    x_hbm,
    w_hbm,
    down,
    upmap,
    cot,
    tenant,
    fill,
    values,
    tgrad,
    te_out,
    tu_out,
    xv,
    wall,
    go,
    va,
    tga,
    tg_v,
    ab_a,
    ab_b,
    send_a,
    vb,
    send_b,
    at,
    recv_b,
    bt,
    gs,
    us,
    usj,
    ur,
    te,
    tu,
    lo,
    ri_s,
    rg_s,
    quarters,
    loc,
    y_sem,
    wy_sem,
    wx_sem,
    wc_sem,
    pa_sem,
    pb_sem,
    gt_sem,
    gu_sem,
):
    f = lax.axis_index("fsdp")
    t = lax.axis_index("tok")
    x = t // 8
    z = (t // 2) % 4
    c = t % 2

    def up(i, d):
        return lax.rem(i + d, 4)

    def dev_y(d):
        return (up(f, d), t)

    def dev_x(d):
        return (f, up(x, d) * 8 + z * 2 + c)

    def dev_z(d):
        return (f, x * 8 + up(z, d) * 2 + c)

    sibling = (f, x * 8 + z * 2 + (1 - c))

    def remote(src, dst, sem, i, dev):
        return pltpu.make_async_remote_copy(
            src_ref=src,
            dst_ref=dst,
            send_sem=sem.at[0, i],
            recv_sem=sem.at[1, i],
            device_id=dev,
            device_id_type=pl.DeviceIdType.MESH,
        )

    def my_cols(i, n):
        return pl.ds(pl.multiple_of(i * n, n), n)

    barrier = pltpu.get_barrier_semaphore()
    for d in (1, 3):
        pl.semaphore_signal(
            barrier, inc=1, device_id=dev_y(d), device_id_type=pl.DeviceIdType.MESH
        )

    def greet(d, carry):
        pl.semaphore_signal(
            barrier,
            inc=1,
            device_id=(f, lax.rem(t + d, 32)),
            device_id_type=pl.DeviceIdType.MESH,
        )
        return carry

    lax.fori_loop(1, 32, greet, 0)

    get_x = pltpu.make_async_copy(x_hbm, xv, loc.at[0])
    get_w = pltpu.make_async_copy(w_hbm, wall.at[f], loc.at[1])
    get_x.start()
    get_w.start()

    def quarter_step(i, carry):
        for k in range(4):
            quarters[4 * i + k] = i
        return carry

    lax.fori_loop(0, 64, quarter_step, 0)

    side = jnp.zeros((16, 16, 128), F32)
    for g in range(4):
        place = pick(iota((32, 128), 1) == iota((32, 128), 0) + 32 * g)
        moved = mm(upmap[...], place, TN).reshape(16, 64, 128)
        side = side + moved[:, g * 16 : (g + 1) * 16, :]
    ab_b[pl.ds(f * 16, 16)] = side.astype(BF)

    pl.semaphore_wait(barrier, 33)

    pending = []

    def ring_y(part_of, sem, n0):
        first = {}
        last = []

        def start():
            for i, (d, s) in enumerate(((1, 0), (3, 1), (1, 1), (3, 0))):
                cp = remote(part_of(f, s), part_of(f, s), sem, n0 + i, dev_y(d))
                cp.start()
                first[d, s] = cp
                pending.append(cp)

        def forward():
            for i, (d, s) in enumerate(((1, 0), (3, 1))):
                first[d, s].wait_recv()
                src = up(f, 4 - d)
                cp = remote(
                    part_of(src, s), part_of(src, s), sem, n0 + 4 + i, dev_y(d)
                )
                cp.start()
                last.append(cp)
                pending.append(cp)

        def near():
            first[1, 1].wait_recv()
            first[3, 0].wait_recv()

        def far():
            for cp in last:
                cp.wait_recv()

        return start, forward, near, far

    b_start, b_forward, b_near, b_far = ring_y(
        lambda i, s: ab_b.at[pl.ds(i * 16 + s * 8, 8)], y_sem, 0
    )
    a_start, a_forward, a_near, a_far = ring_y(
        lambda i, s: ab_a.at[pl.ds(i * 64 + s * 32, 32)], y_sem, 6
    )
    t_start, t_forward, t_near, t_far = ring_y(
        lambda i, s: te.at[i, pl.ds(s * 512, 512)], y_sem, 12
    )
    u_start, u_forward, u_near, u_far = ring_y(
        lambda i, s: tu.at[i, pl.ds(s * 128, 128)], y_sem, 18
    )
    b_start()

    base = (x * 1024 + c * 512, 4096 + z * 1024 + c * 512)
    plane = (dev_x, dev_z)

    def wslice(fi, row0):
        return wall.at[fi, pl.ds(pl.multiple_of(row0, 256), 256), :]

    wy = {}
    n_y = 0

    def wy_start(h):
        nonlocal n_y
        for d, s in ((1, 0), (3, 1), (1, 1), (3, 0)):
            r0 = base[h] + s * 256
            cp = remote(
                w_hbm.at[pl.ds(pl.multiple_of(r0, 256), 256), :],
                wslice(f, r0),
                wy_sem,
                n_y,
                dev_y(d),
            )
            cp.start()
            wy[h, d, s] = cp
            pending.append(cp)
            n_y += 1

    wy_start(0)
    ab_a[pl.ds(f * 64, 64)] = down[...].astype(F32).T.astype(BF).reshape(64, 16, 256)

    b0 = (f * 32 + t) * 2

    def used_rows():
        rows = iota((256, 1), 0)
        return rows < jnp.where(rows < BLOCK, fill[b0], fill[b0 + 1] + BLOCK)

    used = used_rows()
    for j in range(4):
        go[j] = jnp.where(used, cot[:, j * 256 : (j + 1) * 256].astype(F32), 0.0).astype(BF)

    b_forward()
    va[...] = jnp.zeros_like(va)
    b_near()

    wx = {}
    wc = {}
    fw = {}
    counters = {"x": 0, "c": 0}
    foreign = (up(f, 3), up(f, 1), up(f, 2))

    def same_place(fi, r0, sem, kind, dev):
        cp = remote(wslice(fi, r0), wslice(fi, r0), sem, counters[kind], dev)
        counters[kind] += 1
        cp.start()
        pending.append(cp)
        return cp

    def to_sibling(fi, r0, key):
        wc[key] = same_place(fi, r0, wc_sem, "c", sibling)

    def to_plane(fi, r0, d, key, h):
        wx[key] = same_place(fi, r0, wx_sem, "x", plane[h](d))

    def w_near(h):
        nonlocal n_y
        for d, s in ((1, 0), (3, 1)):
            wy[h, d, s].wait_recv()
            src = up(f, 4 - d)
            r0 = base[h] + s * 256
            cp = remote(wslice(src, r0), wslice(src, r0), wy_sem, n_y, dev_y(d))
            n_y += 1
            cp.start()
            fw[h, s] = cp
            pending.append(cp)
        for d, s in ((1, 0), (3, 1), (1, 1), (3, 0)):
            if (d, s) in ((1, 1), (3, 0)):
                wy[h, d, s].wait_recv()
            fi = 0 if d == 1 else 1
            r0 = base[h] + s * 256
            for dd in (1, 3) if s == 0 else (3, 1):
                to_plane(foreign[fi], r0, dd, (h, dd, fi, s), h)
            to_sibling(foreign[fi], r0, (h, 0, fi, s))

    def w_far(h):
        for s in range(2):
            fw[h, s].wait_recv()
            r0 = base[h] + s * 256
            for dd in (1, 3) if s == 0 else (3, 1):
                to_plane(foreign[2], r0, dd, (h, dd, 2, s), h)
            to_sibling(foreign[2], r0, (h, 0, 2, s))

    def here(h, d):
        if h == 0:
            return up(x, d) * 1024 + c * 512
        return 4096 + up(z, d) * 1024 + c * 512

    def w_along(h, fi):
        for d, s in ((1, 0), (3, 1)):
            wx[h, d, fi, s].wait_recv()
            r0 = here(h, 4 - d) + s * 256
            to_plane(foreign[fi], r0, d, (h, 2, fi, s), h)
            to_sibling(foreign[fi], r0, (h, d, fi, s))
        for d, s in ((1, 1), (3, 0)):
            wx[h, d, fi, s].wait_recv()
            r0 = here(h, 4 - d) + s * 256
            to_sibling(foreign[fi], r0, (h, d, fi, s))

    def w_end(h, fi):
        for s in range(2):
            wx[h, 2, fi, s].wait_recv()
            to_sibling(foreign[fi], here(h, 2) + s * 256, (h, 2, fi, s))

    b_far()

    lane32 = iota((16, 128), 1) >> 5
    el = iota((128, 128), 0)
    ej = iota((128, 128), 1)

    def pick_b(i, carry):
        for j in range(2):
            g = tenant[f * 64 + 2 * i + j]
            quarter = quarters[g]
            v = ab_b[quarter]
            vb[j, my_cols(i, 16), :] = jnp.where(
                lane32 == g - 4 * quarter, v.astype(F32), 0.0
            ).astype(BF)
        return carry

    def lanes(i, j):
        return pick((el == i * 32 + (ej & 31)) & ((ej >> 5) == j))

    def pick_a(b, carry):
        send_a[my_cols(b, 16), :] = ab_a[tenant[f * 64 + b]]
        return carry

    def swap_a(d):
        to = lax.rem(t + d, 32)
        return remote(
            send_a.at[my_cols(to, 32), :], at.at[:, my_cols(t, 256)], pa_sem, d, (f, to)
        )

    def swap_b(d):
        to = lax.rem(t + d, 32)
        return remote(send_b.at[to], recv_b.at[t // 4, t % 4], pb_sem, d, (f, to))

    def back_t(d):
        to = lax.rem(t + d, 32)
        return remote(
            gs.at[:, my_cols(to, 256)], te.at[f, my_cols(t, 32), :], gt_sem, d, (f, to)
        )

    def back_u(d):
        to = lax.rem(t + d, 32)
        return remote(
            us.at[to // 4, to % 4], ur.at[t // 4, t % 4], gu_sem, d, (f, to)
        )

    def over_tok(copy, act):
        def step(d, carry):
            cp = copy(d)
            if act == "start":
                cp.start()
            elif act == "recv":
                cp.wait_recv()
            else:
                cp.wait_send()
            return carry

        lax.fori_loop(1, 32, step, 0)

    lax.fori_loop(0, 32, pick_b, 0)
    for j in range(2):
        spread = pick(((el & 31) == (ej & 31)) & ((ej >> 5) == j))
        moved = mm(vb[j], spread)
        side = moved if j == 0 else side + moved
    send_b[...] = side.astype(BF).reshape(32, 16, 128)
    over_tok(swap_b, "start")
    recv_b[t // 4, t % 4] = send_b[t]

    wy_start(1)
    get_x.wait()
    w_near(0)

    over_tok(swap_b, "recv")
    for j in range(2):
        total = jnp.zeros((128, 128), F32)
        for i in range(4):
            total = total + mm(recv_b[:, i].reshape(128, 128), lanes(j, i))
        for q in range(8):
            bt[j * 16 : (j + 1) * 16, q * 128 : (q + 1) * 128] = total[
                q * 16 : (q + 1) * 16, :
            ].astype(BF)
    diagonal = (iota((256, 32), 0) >> 7) == (iota((256, 32), 1) >> 4)
    rank_grad = jnp.zeros((256, 32), F32)
    for j in range(4):
        rank_grad = rank_grad + mm(go[j], bt[:, j * 256 : (j + 1) * 256], NT)
    rg_s[...] = jnp.where(diagonal, SCALE * rank_grad, 0.0).astype(BF)

    def terms_step(k, carry):
        cols = my_cols(k, 1024)
        gs[:, cols] = mm(rg_s[...], xv[:, cols], TN).astype(BF)
        return carry

    lax.fori_loop(0, 8, terms_step, 0)
    over_tok(back_t, "start")
    te[f, my_cols(t, 32), :] = gs[:, my_cols(t, 256)]

    w_near(1)
    a_start()
    get_w.wait()

    def own_step(k, carry):
        cols = my_cols(k, 256)
        wk = wall[f, cols, :]
        va[f] += mm(xv[:, cols], wk)
        tga[:, cols] = mm(go[f], wk, NT)
        return carry

    lax.fori_loop(0, 8, own_step, 0)
    for h in range(2):
        w_far(h)
    over_tok(back_t, "recv")
    put_own = pltpu.make_async_copy(te.at[f], te_out.at[f], loc.at[3])
    put_own.start()
    w_along(0, 0)
    a_forward()
    w_along(1, 0)
    a_near()
    t_start()
    lax.fori_loop(8, 20, own_step, 0)
    a_far()
    lax.fori_loop(0, 64, pick_a, 0)
    over_tok(swap_a, "start")
    at[:, my_cols(t, 256)] = send_a[my_cols(t, 32), :]
    w_along(0, 1)
    w_along(1, 1)
    early = len(pending)
    t_forward()
    lax.fori_loop(20, 32, own_step, 0)

    over_tok(swap_a, "recv")

    def rank_step(k, total):
        cols = my_cols(k, 1024)
        return total + mm(xv[:, cols], at[:, cols], NT)

    rank_in = lax.fori_loop(0, 8, rank_step, jnp.zeros((256, 32), F32))
    ri_s[...] = jnp.where(diagonal, rank_in, 0.0).astype(BF)
    for k in range(4):
        part = (SCALE * mm(ri_s[...], go[k], TN)).astype(BF)
        for q in range(2):
            for j in range(2):
                usj[j, (2 * k + q) * 16 : (2 * k + q + 1) * 16, :] = part[
                    j * 16 : (j + 1) * 16, q * 128 : (q + 1) * 128
                ]
    for i in range(4):
        part = mm(usj[0], lanes(i, 0)) + mm(usj[1], lanes(i, 1))
        us[:, i] = part.astype(BF).reshape(8, 16, 128)
    over_tok(back_u, "start")
    w_end(0, 0)
    w_end(1, 0)
    ur[t // 4, t % 4] = us[t // 4, t % 4]

    for j in range(4):
        lo[:, j * 256 : (j + 1) * 256] = (
            SCALE * mm(ri_s[...], bt[:, j * 256 : (j + 1) * 256])
        ).astype(BF)
    def tile(row0, shards, last):
        cols = pl.ds(pl.multiple_of(row0, 256), 256)
        xk = xv[:, cols]
        total = tga[:, cols]
        if last:
            total = total + mm(rg_s[...], at[:, cols])
        for fi in shards:
            wk = wall[fi, cols, :]
            va[fi] += mm(xk, wk)
            total = total + mm(go[fi], wk, NT)
        if not last:
            tga[:, cols] = total
            return
        tg_v[:, cols] = total.astype(BF)
        pltpu.make_async_copy(tg_v.at[:, cols], tgrad.at[:, cols], loc.at[2]).start()

    def tiles(d, shards=foreign, last=True):
        def step(i, carry):
            h = i // 4
            pos = jnp.where(h == 0, lax.rem(x + d, 4), lax.rem(z + d, 4))
            tile(h * 4096 + pos * 1024 + (i % 4) * 256, shards, last)
            return carry

        lax.fori_loop(0, 8, step, 0)

    def await_sibling(d, shards=range(3)):
        for h in range(2):
            for fi in shards:
                for s in range(2):
                    wc[h, d, fi, s].wait_recv()

    over_tok(back_u, "recv")
    for j in range(2):
        packed = jnp.zeros((128, 128), F32)
        for q in range(4):
            packed = packed + mm(ur[2 * q : 2 * q + 2].reshape(128, 128), lanes(j, q))
        tu[f, j * 128 : (j + 1) * 128, :] = packed.astype(BF)
    u_start()
    w_along(0, 2)
    w_along(1, 2)
    await_sibling(0)
    tiles(0)
    w_end(0, 1)
    w_end(1, 1)
    u_forward()
    await_sibling(1)
    tiles(3)
    t_near()
    puts = [put_own]
    for i, fi in enumerate(foreign[:2]):
        puts.append(pltpu.make_async_copy(te.at[fi], te_out.at[fi], loc.at[4 + i]))
        puts[-1].start()
    w_end(0, 2)
    w_end(1, 2)
    await_sibling(3)
    tiles(1)
    await_sibling(2, (0, 1))
    tiles(2, foreign[:2], False)
    for copy in (swap_a, swap_b, back_t, back_u):
        over_tok(copy, "sent")
    for cp in pending[:early]:
        cp.wait_send()
    await_sibling(2, (2,))
    tiles(2, foreign[2:])
    used = used_rows()
    for j in range(4):
        cols = slice(j * 256, (j + 1) * 256)
        values[:, cols] = jnp.where(used, va[j] + lo[:, cols].astype(F32), 0.0).astype(BF)
    t_far()
    puts.append(pltpu.make_async_copy(te.at[foreign[2]], te_out.at[foreign[2]], loc.at[6]))
    puts[-1].start()
    u_near()
    u_far()
    puts.append(pltpu.make_async_copy(tu, tu_out, loc.at[7]))
    puts[-1].start()

    pltpu.make_async_copy(tg_v, tgrad, loc.at[2]).wait()
    for cp in pending[early:]:
        cp.wait_send()
    for cp in puts:
        cp.wait()


def sums(v_in, t_in, te_in, tu_in, tenant, fill, v_out, t_out, gdown, gup, *scratch):
    v_s, t_s, te, tu, acc, accu, cnt, mine, sem = scratch
    first = [
        pltpu.make_async_copy(te_in, te, sem.at[0, 9]),
        pltpu.make_async_copy(tu_in, tu, sem.at[0, 10]),
    ]
    moves = [(v_in, v_s, v_out)]
    for i in range(8):
        rows = pl.ds(i * 32, 32)
        moves.append((t_in.at[rows, :], t_s.at[rows, :], t_out.at[rows, :]))
    loads = [pltpu.make_async_copy(a, b, sem.at[0, i]) for i, (a, b, _) in enumerate(moves)]
    stores = [pltpu.make_async_copy(b, c, sem.at[1, i]) for i, (_, b, c) in enumerate(moves)]
    for cp in first + loads:
        cp.start()
    f = lax.axis_index("fsdp")
    acc[...] = jnp.zeros_like(acc)
    accu[...] = jnp.zeros_like(accu)

    def clear(i, carry):
        cnt[i] = 0
        return carry

    lax.fori_loop(0, 65, clear, 0)

    def note(b, n):
        g = tenant[b] - f * 64
        own = (g >= 0) & (g < 64)
        slot = jnp.where(own, g, 64)
        cnt[slot] = cnt[slot] + fill[b]
        mine[n] = b
        return n + jnp.where(own, 1, 0)

    count = lax.fori_loop(0, 256, note, 0)
    lane32 = iota((16, 128), 1) >> 5
    for cp in first:
        cp.wait()
    for cp, out in zip(loads, stores):
        cp.wait()
        out.start()

    def add(i, carry):
        b = mine[i]
        slot = tenant[b] - f * 64
        fi = b // 64
        k = b % 64
        acc[slot] += te[fi, k].astype(F32)
        accu[slot] += jnp.where(lane32 == k // 16, tu[fi, (k % 2) * 8 + (k % 16) // 2].astype(F32), 0.0)
        return carry

    lax.fori_loop(0, count, add, 0)

    def mean(i, carry):
        n = jnp.maximum(cnt[i].astype(F32), 1.0)
        acc[i] = acc[i] / n
        accu[i] = accu[i] / n
        return carry

    lax.fori_loop(0, 64, mean, 0, unroll=4)
    for k in range(8):
        cols = slice(k * 128, (k + 1) * 128)
        gdown[:, cols] = acc[k * 8 : (k + 1) * 8].reshape(128, 256).T
        ut = accu[k * 8 : (k + 1) * 8].reshape(128, 128).T
        gup[:, cols] = ut[0:32] + ut[32:64] + ut[64:96] + ut[96:128]
    for cp in stores:
        cp.wait()


def local(tokens, weight, down, up, cotangent, tenant, fill):
    any_ = pl.BlockSpec(memory_space=pl.ANY)
    vmem = pl.BlockSpec(memory_space=pltpu.VMEM)
    smem = pl.BlockSpec(memory_space=pltpu.SMEM)
    dma = pltpu.SemaphoreType.DMA
    V = pltpu.VMEM
    v_shape = jax.ShapeDtypeStruct((256, 1024), BF)
    t_shape = jax.ShapeDtypeStruct((256, 8192), BF)
    v, tg, te, tu = pl.pallas_call(
        kernel,
        out_shape=(
            v_shape,
            t_shape,
            jax.ShapeDtypeStruct((4, 1024, 256), BF),
            jax.ShapeDtypeStruct((4, 256, 128), BF),
        ),
        in_specs=[any_, any_, vmem, vmem, vmem, smem, smem],
        out_specs=(vmem, any_, any_, any_),
        scratch_shapes=[
            V((256, 8192), BF),
            V((4, 8192, 256), BF),
            V((4, 256, 256), BF),
            V((4, 256, 256), F32),
            V((256, 8192), F32),
            V((256, 8192), BF),
            V((256, 16, 256), BF),
            V((64, 16, 128), BF),
            V((1024, 256), BF),
            V((2, 512, 128), BF),
            V((32, 16, 128), BF),
            V((32, 8192), BF),
            V((8, 4, 16, 128), BF),
            V((32, 1024), BF),
            V((32, 8192), BF),
            V((8, 4, 16, 128), BF),
            V((2, 128, 128), BF),
            V((8, 4, 16, 128), BF),
            V((4, 1024, 256), BF),
            V((4, 256, 128), BF),
            V((256, 1024), BF),
            V((256, 32), BF),
            V((256, 32), BF),
            pltpu.SMEM((256,), jnp.int32),
            dma((8,)),
            dma((2, 24)),
            dma((2, 12)),
            dma((2, 36)),
            dma((2, 48)),
            dma((2, 32)),
            dma((2, 32)),
            dma((2, 32)),
            dma((2, 32)),
        ],
        compiler_params=pltpu.CompilerParams(
            has_side_effects=True, collective_id=1, vmem_limit_bytes=60 * 1024 * 1024
        ),
        cost_estimate=pl.CostEstimate(
            flops=9_000_000_000, bytes_accessed=30_000_000, transcendentals=0
        ),
    )(tokens, weight, down, up, cotangent, tenant, fill)
    return pl.pallas_call(
        sums,
        out_shape=(
            v_shape,
            t_shape,
            jax.ShapeDtypeStruct((256, 1024), F32),
            jax.ShapeDtypeStruct((32, 1024), F32),
        ),
        in_specs=[any_, any_, any_, any_, smem, smem],
        out_specs=(any_, any_, vmem, vmem),
        scratch_shapes=[
            V((256, 1024), BF),
            V((256, 8192), BF),
            V((4, 64, 16, 256), BF),
            V((4, 16, 16, 128), BF),
            V((65, 16, 256), F32),
            V((65, 16, 128), F32),
            pltpu.SMEM((65,), jnp.int32),
            pltpu.SMEM((256,), jnp.int32),
            dma((2, 11)),
        ],
        compiler_params=pltpu.CompilerParams(vmem_limit_bytes=60 * 1024 * 1024),
    )(v, tg, te.reshape(4, 64, 16, 256), tu.reshape(4, 16, 16, 128), tenant, fill)


def solution(mesh):
    placed = (
        P(("fsdp", "tok"), None),
        P(None, "fsdp"),
        P("tok", "fsdp"),
        P("tok", "fsdp"),
        P(("fsdp", "tok"), None),
        P(),
        P(),
    )
    return jax.shard_map(
        local,
        mesh=mesh,
        in_specs=placed,
        out_specs=(
            P(("fsdp", "tok"), None),
            P(("fsdp", "tok"), None),
            P("tok", "fsdp"),
            P("tok", "fsdp"),
        ),
        check_vma=False,
    )
```

```python
import jax
import jax.numpy as jnp
from jax import lax
from jax.experimental import pallas as pl
from jax.experimental.pallas import tpu as pltpu
from jax.sharding import PartitionSpec as P

RANK = 16
BLOCK = 128
SCALE = 2.0
BF = jnp.bfloat16
F32 = jnp.float32
NT = (((1,), (1,)), ((), ()))
TN = (((0,), (0,)), ((), ()))


def mm(a, b, dims=(((1,), (0,)), ((), ()))):
    return lax.dot_general(a, b, dims, preferred_element_type=F32)


def iota(shape, dim):
    return lax.broadcasted_iota(jnp.int32, shape, dim)


def pick(cond):
    return jnp.where(cond, 1.0, 0.0).astype(BF)


def kernel(
    x_hbm,
    w_hbm,
    down,
    upmap,
    cot,
    tenant,
    fill,
    values,
    tgrad,
    te_out,
    tu_out,
    xv,
    wall,
    go,
    va,
    tga,
    tg_v,
    ab_a,
    ab_b,
    send_a,
    vb,
    send_b,
    at,
    recv_b,
    bt,
    gs,
    us,
    usj,
    ur,
    te,
    tu,
    lo,
    ri_s,
    rg_s,
    quarters,
    loc,
    y_sem,
    wy_sem,
    wx_sem,
    wc_sem,
    pa_sem,
    pb_sem,
    gt_sem,
    gu_sem,
):
    f = lax.axis_index("fsdp")
    t = lax.axis_index("tok")
    x = t // 8
    z = (t // 2) % 4
    c = t % 2

    def up(i, d):
        return lax.rem(i + d, 4)

    def dev_y(d):
        return (up(f, d), t)

    def dev_x(d):
        return (f, up(x, d) * 8 + z * 2 + c)

    def dev_z(d):
        return (f, x * 8 + up(z, d) * 2 + c)

    sibling = (f, x * 8 + z * 2 + (1 - c))

    def remote(src, dst, sem, i, dev):
        return pltpu.make_async_remote_copy(
            src_ref=src,
            dst_ref=dst,
            send_sem=sem.at[0, i],
            recv_sem=sem.at[1, i],
            device_id=dev,
            device_id_type=pl.DeviceIdType.MESH,
        )

    def my_cols(i, n):
        return pl.ds(pl.multiple_of(i * n, n), n)

    barrier = pltpu.get_barrier_semaphore()
    for d in (1, 3):
        pl.semaphore_signal(
            barrier, inc=1, device_id=dev_y(d), device_id_type=pl.DeviceIdType.MESH
        )

    def greet(d, carry):
        pl.semaphore_signal(
            barrier,
            inc=1,
            device_id=(f, lax.rem(t + d, 32)),
            device_id_type=pl.DeviceIdType.MESH,
        )
        return carry

    lax.fori_loop(1, 32, greet, 0)

    get_x = pltpu.make_async_copy(x_hbm, xv, loc.at[0])
    get_w = pltpu.make_async_copy(w_hbm, wall.at[f], loc.at[1])
    get_x.start()
    get_w.start()

    def quarter_step(i, carry):
        for k in range(4):
            quarters[4 * i + k] = i
        return carry

    lax.fori_loop(0, 64, quarter_step, 0)

    side = jnp.zeros((16, 16, 128), F32)
    for g in range(4):
        place = pick(iota((32, 128), 1) == iota((32, 128), 0) + 32 * g)
        moved = mm(upmap[...], place, TN).reshape(16, 64, 128)
        side = side + moved[:, g * 16 : (g + 1) * 16, :]
    ab_b[pl.ds(f * 16, 16)] = side.astype(BF)

    pl.semaphore_wait(barrier, 33)

    pending = []

    def ring_y(part_of, sem, n0):
        first = {}
        last = []

        def start():
            for i, (d, s) in enumerate(((1, 0), (3, 1), (1, 1), (3, 0))):
                cp = remote(part_of(f, s), part_of(f, s), sem, n0 + i, dev_y(d))
                cp.start()
                first[d, s] = cp
                pending.append(cp)

        def forward():
            for i, (d, s) in enumerate(((1, 0), (3, 1))):
                first[d, s].wait_recv()
                src = up(f, 4 - d)
                cp = remote(
                    part_of(src, s), part_of(src, s), sem, n0 + 4 + i, dev_y(d)
                )
                cp.start()
                last.append(cp)
                pending.append(cp)

        def near():
            first[1, 1].wait_recv()
            first[3, 0].wait_recv()

        def far():
            for cp in last:
                cp.wait_recv()

        return start, forward, near, far

    b_start, b_forward, b_near, b_far = ring_y(
        lambda i, s: ab_b.at[pl.ds(i * 16 + s * 8, 8)], y_sem, 0
    )
    a_start, a_forward, a_near, a_far = ring_y(
        lambda i, s: ab_a.at[pl.ds(i * 64 + s * 32, 32)], y_sem, 6
    )
    t_start, t_forward, t_near, t_far = ring_y(
        lambda i, s: te.at[i, pl.ds(s * 512, 512)], y_sem, 12
    )
    u_start, u_forward, u_near, u_far = ring_y(
        lambda i, s: tu.at[i, pl.ds(s * 128, 128)], y_sem, 18
    )
    b_start()

    base = (x * 1024 + c * 512, 4096 + z * 1024 + c * 512)
    plane = (dev_x, dev_z)

    def wslice(fi, row0):
        return wall.at[fi, pl.ds(pl.multiple_of(row0, 256), 256), :]

    wy = {}
    n_y = 0

    def wy_start(h):
        nonlocal n_y
        for d, s in ((1, 0), (3, 1), (1, 1), (3, 0)):
            r0 = base[h] + s * 256
            cp = remote(
                w_hbm.at[pl.ds(pl.multiple_of(r0, 256), 256), :],
                wslice(f, r0),
                wy_sem,
                n_y,
                dev_y(d),
            )
            cp.start()
            wy[h, d, s] = cp
            pending.append(cp)
            n_y += 1

    wy_start(0)
    ab_a[pl.ds(f * 64, 64)] = down[...].astype(F32).T.astype(BF).reshape(64, 16, 256)

    b0 = (f * 32 + t) * 2

    def used_rows():
        rows = iota((256, 1), 0)
        return rows < jnp.where(rows < BLOCK, fill[b0], fill[b0 + 1] + BLOCK)

    used = used_rows()
    for j in range(4):
        go[j] = jnp.where(used, cot[:, j * 256 : (j + 1) * 256].astype(F32), 0.0).astype(BF)

    b_forward()
    va[...] = jnp.zeros_like(va)
    b_near()

    wx = {}
    wc = {}
    fw = {}
    counters = {"x": 0, "c": 0}
    foreign = (up(f, 3), up(f, 1), up(f, 2))

    def same_place(fi, r0, sem, kind, dev):
        cp = remote(wslice(fi, r0), wslice(fi, r0), sem, counters[kind], dev)
        counters[kind] += 1
        cp.start()
        pending.append(cp)
        return cp

    def to_sibling(fi, r0, key):
        wc[key] = same_place(fi, r0, wc_sem, "c", sibling)

    def to_plane(fi, r0, d, key, h):
        wx[key] = same_place(fi, r0, wx_sem, "x", plane[h](d))

    def w_near(h):
        nonlocal n_y
        for d, s in ((1, 0), (3, 1)):
            wy[h, d, s].wait_recv()
            src = up(f, 4 - d)
            r0 = base[h] + s * 256
            cp = remote(wslice(src, r0), wslice(src, r0), wy_sem, n_y, dev_y(d))
            n_y += 1
            cp.start()
            fw[h, s] = cp
            pending.append(cp)
        for d, s in ((1, 0), (3, 1), (1, 1), (3, 0)):
            if (d, s) in ((1, 1), (3, 0)):
                wy[h, d, s].wait_recv()
            fi = 0 if d == 1 else 1
            r0 = base[h] + s * 256
            for dd in (1, 3) if s == 0 else (3, 1):
                to_plane(foreign[fi], r0, dd, (h, dd, fi, s), h)
            to_sibling(foreign[fi], r0, (h, 0, fi, s))

    def w_far(h):
        for s in range(2):
            fw[h, s].wait_recv()
            r0 = base[h] + s * 256
            for dd in (1, 3) if s == 0 else (3, 1):
                to_plane(foreign[2], r0, dd, (h, dd, 2, s), h)
            to_sibling(foreign[2], r0, (h, 0, 2, s))

    def here(h, d):
        if h == 0:
            return up(x, d) * 1024 + c * 512
        return 4096 + up(z, d) * 1024 + c * 512

    def w_along(h, fi):
        for d, s in ((1, 0), (3, 1)):
            wx[h, d, fi, s].wait_recv()
            r0 = here(h, 4 - d) + s * 256
            to_plane(foreign[fi], r0, d, (h, 2, fi, s), h)
            to_sibling(foreign[fi], r0, (h, d, fi, s))
        for d, s in ((1, 1), (3, 0)):
            wx[h, d, fi, s].wait_recv()
            r0 = here(h, 4 - d) + s * 256
            to_sibling(foreign[fi], r0, (h, d, fi, s))

    def w_end(h, fi):
        for s in range(2):
            wx[h, 2, fi, s].wait_recv()
            to_sibling(foreign[fi], here(h, 2) + s * 256, (h, 2, fi, s))

    b_far()

    lane32 = iota((16, 128), 1) >> 5
    el = iota((128, 128), 0)
    ej = iota((128, 128), 1)

    def pick_b(i, carry):
        for j in range(2):
            g = tenant[f * 64 + 2 * i + j]
            quarter = quarters[g]
            v = ab_b[quarter]
            vb[j, my_cols(i, 16), :] = jnp.where(
                lane32 == g - 4 * quarter, v.astype(F32), 0.0
            ).astype(BF)
        return carry

    def lanes(i, j):
        return pick((el == i * 32 + (ej & 31)) & ((ej >> 5) == j))

    def pick_a(b, carry):
        send_a[my_cols(b, 16), :] = ab_a[tenant[f * 64 + b]]
        return carry

    def swap_a(d):
        to = lax.rem(t + d, 32)
        return remote(
            send_a.at[my_cols(to, 32), :], at.at[:, my_cols(t, 256)], pa_sem, d, (f, to)
        )

    def swap_b(d):
        to = lax.rem(t + d, 32)
        return remote(send_b.at[to], recv_b.at[t // 4, t % 4], pb_sem, d, (f, to))

    def back_t(d):
        to = lax.rem(t + d, 32)
        return remote(
            gs.at[:, my_cols(to, 256)], te.at[f, my_cols(t, 32), :], gt_sem, d, (f, to)
        )

    def back_u(d):
        to = lax.rem(t + d, 32)
        return remote(
            us.at[to // 4, to % 4], ur.at[t // 4, t % 4], gu_sem, d, (f, to)
        )

    def over_tok(copy, act):
        def step(d, carry):
            cp = copy(d)
            if act == "start":
                cp.start()
            elif act == "recv":
                cp.wait_recv()
            else:
                cp.wait_send()
            return carry

        lax.fori_loop(1, 32, step, 0)

    lax.fori_loop(0, 32, pick_b, 0)
    for j in range(2):
        spread = pick(((el & 31) == (ej & 31)) & ((ej >> 5) == j))
        moved = mm(vb[j], spread)
        side = moved if j == 0 else side + moved
    send_b[...] = side.astype(BF).reshape(32, 16, 128)
    over_tok(swap_b, "start")
    recv_b[t // 4, t % 4] = send_b[t]

    wy_start(1)
    get_x.wait()
    w_near(0)

    over_tok(swap_b, "recv")
    for j in range(2):
        total = jnp.zeros((128, 128), F32)
        for i in range(4):
            total = total + mm(recv_b[:, i].reshape(128, 128), lanes(j, i))
        for q in range(8):
            bt[j * 16 : (j + 1) * 16, q * 128 : (q + 1) * 128] = total[
                q * 16 : (q + 1) * 16, :
            ].astype(BF)
    diagonal = (iota((256, 32), 0) >> 7) == (iota((256, 32), 1) >> 4)
    rank_grad = jnp.zeros((256, 32), F32)
    for j in range(4):
        rank_grad = rank_grad + mm(go[j], bt[:, j * 256 : (j + 1) * 256], NT)
    rg_s[...] = jnp.where(diagonal, SCALE * rank_grad, 0.0).astype(BF)

    def terms_step(k, carry):
        cols = my_cols(k, 1024)
        gs[:, cols] = mm(rg_s[...], xv[:, cols], TN).astype(BF)
        return carry

    lax.fori_loop(0, 8, terms_step, 0)
    over_tok(back_t, "start")
    te[f, my_cols(t, 32), :] = gs[:, my_cols(t, 256)]

    w_near(1)
    a_start()
    get_w.wait()

    def own_step(k, carry):
        cols = my_cols(k, 256)
        wk = wall[f, cols, :]
        va[f] += mm(xv[:, cols], wk)
        tga[:, cols] = mm(go[f], wk, NT)
        return carry

    lax.fori_loop(0, 8, own_step, 0)
    for h in range(2):
        w_far(h)
    over_tok(back_t, "recv")
    put_own = pltpu.make_async_copy(te.at[f], te_out.at[f], loc.at[3])
    put_own.start()
    w_along(0, 0)
    a_forward()
    w_along(1, 0)
    a_near()
    t_start()
    lax.fori_loop(8, 20, own_step, 0)
    a_far()
    lax.fori_loop(0, 64, pick_a, 0)
    over_tok(swap_a, "start")
    at[:, my_cols(t, 256)] = send_a[my_cols(t, 32), :]
    w_along(0, 1)
    w_along(1, 1)
    t_forward()
    lax.fori_loop(20, 32, own_step, 0)

    over_tok(swap_a, "recv")

    def rank_step(k, total):
        cols = my_cols(k, 1024)
        return total + mm(xv[:, cols], at[:, cols], NT)

    rank_in = lax.fori_loop(0, 8, rank_step, jnp.zeros((256, 32), F32))
    ri_s[...] = jnp.where(diagonal, rank_in, 0.0).astype(BF)
    for k in range(4):
        part = (SCALE * mm(ri_s[...], go[k], TN)).astype(BF)
        for q in range(2):
            for j in range(2):
                usj[j, (2 * k + q) * 16 : (2 * k + q + 1) * 16, :] = part[
                    j * 16 : (j + 1) * 16, q * 128 : (q + 1) * 128
                ]
    for i in range(4):
        part = mm(usj[0], lanes(i, 0)) + mm(usj[1], lanes(i, 1))
        us[:, i] = part.astype(BF).reshape(8, 16, 128)
    over_tok(back_u, "start")
    w_end(0, 0)
    w_end(1, 0)
    ur[t // 4, t % 4] = us[t // 4, t % 4]

    for j in range(4):
        lo[:, j * 256 : (j + 1) * 256] = (
            SCALE * mm(ri_s[...], bt[:, j * 256 : (j + 1) * 256])
        ).astype(BF)
    def tile(row0):
        cols = pl.ds(pl.multiple_of(row0, 256), 256)
        xk = xv[:, cols]
        total = tga[:, cols] + mm(rg_s[...], at[:, cols])
        for fi in foreign:
            wk = wall[fi, cols, :]
            va[fi] += mm(xk, wk)
            total = total + mm(go[fi], wk, NT)
        tg_v[:, cols] = total.astype(BF)
        pltpu.make_async_copy(tg_v.at[:, cols], tgrad.at[:, cols], loc.at[2]).start()

    def tiles(d):
        def step(i, carry):
            h = i // 4
            pos = jnp.where(h == 0, lax.rem(x + d, 4), lax.rem(z + d, 4))
            tile(h * 4096 + pos * 1024 + (i % 4) * 256)
            return carry

        lax.fori_loop(0, 8, step, 0)

    def await_sibling(d):
        for h in range(2):
            for fi in range(3):
                for s in range(2):
                    wc[h, d, fi, s].wait_recv()

    over_tok(back_u, "recv")
    for j in range(2):
        packed = jnp.zeros((128, 128), F32)
        for q in range(4):
            packed = packed + mm(ur[2 * q : 2 * q + 2].reshape(128, 128), lanes(j, q))
        tu[f, j * 128 : (j + 1) * 128, :] = packed.astype(BF)
    u_start()
    w_along(0, 2)
    w_along(1, 2)
    await_sibling(0)
    tiles(0)
    w_end(0, 1)
    w_end(1, 1)
    u_forward()
    await_sibling(1)
    tiles(3)
    t_near()
    puts = [put_own]
    for i, fi in enumerate(foreign[:2]):
        puts.append(pltpu.make_async_copy(te.at[fi], te_out.at[fi], loc.at[4 + i]))
        puts[-1].start()
    w_end(0, 2)
    w_end(1, 2)
    await_sibling(3)
    tiles(1)
    await_sibling(2)
    tiles(2)
    used = used_rows()
    for j in range(4):
        cols = slice(j * 256, (j + 1) * 256)
        values[:, cols] = jnp.where(used, va[j] + lo[:, cols].astype(F32), 0.0).astype(BF)
    t_far()
    puts.append(pltpu.make_async_copy(te.at[foreign[2]], te_out.at[foreign[2]], loc.at[6]))
    puts[-1].start()
    u_near()
    u_far()
    puts.append(pltpu.make_async_copy(tu, tu_out, loc.at[7]))
    puts[-1].start()

    pltpu.make_async_copy(tg_v, tgrad, loc.at[2]).wait()
    for copy in (swap_a, swap_b, back_t, back_u):
        over_tok(copy, "sent")
    for cp in pending:
        cp.wait_send()
    for cp in puts:
        cp.wait()


def sums(v_in, t_in, te_in, tu_in, tenant, fill, v_out, t_out, gdown, gup, *scratch):
    v_s, t_s, te, tu, acc, accu, cnt, mine, sem = scratch
    first = [
        pltpu.make_async_copy(te_in, te, sem.at[0, 9]),
        pltpu.make_async_copy(tu_in, tu, sem.at[0, 10]),
    ]
    moves = [(v_in, v_s, v_out)]
    for i in range(8):
        rows = pl.ds(i * 32, 32)
        moves.append((t_in.at[rows, :], t_s.at[rows, :], t_out.at[rows, :]))
    loads = [pltpu.make_async_copy(a, b, sem.at[0, i]) for i, (a, b, _) in enumerate(moves)]
    stores = [pltpu.make_async_copy(b, c, sem.at[1, i]) for i, (_, b, c) in enumerate(moves)]
    for cp in first + loads:
        cp.start()
    f = lax.axis_index("fsdp")
    acc[...] = jnp.zeros_like(acc)
    accu[...] = jnp.zeros_like(accu)

    def clear(i, carry):
        cnt[i] = 0
        return carry

    lax.fori_loop(0, 65, clear, 0)

    def note(b, n):
        g = tenant[b] - f * 64
        own = (g >= 0) & (g < 64)
        slot = jnp.where(own, g, 64)
        cnt[slot] = cnt[slot] + fill[b]
        mine[n] = b
        return n + jnp.where(own, 1, 0)

    count = lax.fori_loop(0, 256, note, 0)
    lane32 = iota((16, 128), 1) >> 5
    for cp in first:
        cp.wait()

    def add(i, carry):
        b = mine[i]
        slot = tenant[b] - f * 64
        fi = b // 64
        k = b % 64
        acc[slot] += te[fi, k].astype(F32)
        accu[slot] += jnp.where(lane32 == k // 16, tu[fi, (k % 2) * 8 + (k % 16) // 2].astype(F32), 0.0)
        return carry

    lax.fori_loop(0, count // 2, add, 0)
    for cp, out in zip(loads, stores):
        cp.wait()
        out.start()
    lax.fori_loop(count // 2, count, add, 0)

    def mean(i, carry):
        n = jnp.maximum(cnt[i].astype(F32), 1.0)
        acc[i] = acc[i] / n
        accu[i] = accu[i] / n
        return carry

    lax.fori_loop(0, 64, mean, 0, unroll=4)
    for k in range(8):
        cols = slice(k * 128, (k + 1) * 128)
        gdown[:, cols] = acc[k * 8 : (k + 1) * 8].reshape(128, 256).T
        ut = accu[k * 8 : (k + 1) * 8].reshape(128, 128).T
        gup[:, cols] = ut[0:32] + ut[32:64] + ut[64:96] + ut[96:128]
    for cp in stores:
        cp.wait()


def local(tokens, weight, down, up, cotangent, tenant, fill):
    any_ = pl.BlockSpec(memory_space=pl.ANY)
    vmem = pl.BlockSpec(memory_space=pltpu.VMEM)
    smem = pl.BlockSpec(memory_space=pltpu.SMEM)
    dma = pltpu.SemaphoreType.DMA
    V = pltpu.VMEM
    v_shape = jax.ShapeDtypeStruct((256, 1024), BF)
    t_shape = jax.ShapeDtypeStruct((256, 8192), BF)
    v, tg, te, tu = pl.pallas_call(
        kernel,
        out_shape=(
            v_shape,
            t_shape,
            jax.ShapeDtypeStruct((4, 1024, 256), BF),
            jax.ShapeDtypeStruct((4, 256, 128), BF),
        ),
        in_specs=[any_, any_, vmem, vmem, vmem, smem, smem],
        out_specs=(vmem, any_, any_, any_),
        scratch_shapes=[
            V((256, 8192), BF),
            V((4, 8192, 256), BF),
            V((4, 256, 256), BF),
            V((4, 256, 256), F32),
            V((256, 8192), F32),
            V((256, 8192), BF),
            V((256, 16, 256), BF),
            V((64, 16, 128), BF),
            V((1024, 256), BF),
            V((2, 512, 128), BF),
            V((32, 16, 128), BF),
            V((32, 8192), BF),
            V((8, 4, 16, 128), BF),
            V((32, 1024), BF),
            V((32, 8192), BF),
            V((8, 4, 16, 128), BF),
            V((2, 128, 128), BF),
            V((8, 4, 16, 128), BF),
            V((4, 1024, 256), BF),
            V((4, 256, 128), BF),
            V((256, 1024), BF),
            V((256, 32), BF),
            V((256, 32), BF),
            pltpu.SMEM((256,), jnp.int32),
            dma((8,)),
            dma((2, 24)),
            dma((2, 12)),
            dma((2, 36)),
            dma((2, 48)),
            dma((2, 32)),
            dma((2, 32)),
            dma((2, 32)),
            dma((2, 32)),
        ],
        compiler_params=pltpu.CompilerParams(
            has_side_effects=True, collective_id=1, vmem_limit_bytes=60 * 1024 * 1024
        ),
        cost_estimate=pl.CostEstimate(
            flops=9_000_000_000, bytes_accessed=30_000_000, transcendentals=0
        ),
    )(tokens, weight, down, up, cotangent, tenant, fill)
    return pl.pallas_call(
        sums,
        out_shape=(
            v_shape,
            t_shape,
            jax.ShapeDtypeStruct((256, 1024), F32),
            jax.ShapeDtypeStruct((32, 1024), F32),
        ),
        in_specs=[any_, any_, any_, any_, smem, smem],
        out_specs=(any_, any_, vmem, vmem),
        scratch_shapes=[
            V((256, 1024), BF),
            V((256, 8192), BF),
            V((4, 64, 16, 256), BF),
            V((4, 16, 16, 128), BF),
            V((65, 16, 256), F32),
            V((65, 16, 128), F32),
            pltpu.SMEM((65,), jnp.int32),
            pltpu.SMEM((256,), jnp.int32),
            dma((2, 11)),
        ],
        compiler_params=pltpu.CompilerParams(vmem_limit_bytes=60 * 1024 * 1024),
    )(v, tg, te.reshape(4, 64, 16, 256), tu.reshape(4, 16, 16, 128), tenant, fill)


def solution(mesh):
    placed = (
        P(("fsdp", "tok"), None),
        P(None, "fsdp"),
        P("tok", "fsdp"),
        P("tok", "fsdp"),
        P(("fsdp", "tok"), None),
        P(),
        P(),
    )
    return jax.shard_map(
        local,
        mesh=mesh,
        in_specs=placed,
        out_specs=(
            P(("fsdp", "tok"), None),
            P(("fsdp", "tok"), None),
            P("tok", "fsdp"),
            P("tok", "fsdp"),
        ),
        check_vma=False,
    )
```
